32 devices in a mesh: row: 8 (over y, x, core), col: 4 (over z).
Axes of the slice: x: 2, y: 2, z: 4, core: 2. Of those that a mesh axis runs over, the one named last changes fastest.
Arguments:
- reduced_basis: bfloat16 [5, 96, 16384], P(None, None, ('row', 'col')), may hold values from -6 to 6
- cell_jacobian: float32 [5, 5, 16384], P(None, None, ('row', 'col')), may hold values from -4 to 4
- face_cells: int32 [2, 32768], P(None, ('row', 'col')), may hold values from 0 to 511, as said below
- face_jacobian: float32 [2, 5, 5, 32768], P(None, None, None, ('row', 'col')), may hold values from -3 to 3
- limiter_flags: int32 [32768], P(('row', 'col')), may hold values 0 or 1
- viscosity: float32 [5], replicated, may hold values from 0.1 to 1
- ghost_cells: int32 [5120], P(('row', 'col')), may hold values from 0 to 511
- ghost_jacobian: float32 [5, 5, 5120], P(None, None, ('row', 'col')), may hold values from -3 to 3
- ghost_counts: int32 [256], P(('row', 'col')), may hold values from 4 to 32, as said below
- receive_cells: int32 [5120], P(('row', 'col')), may hold values from 0 to 511
- coordinates: float32 [96], replicated, may hold values from -5 to 5
- base_residual: float32 [5, 16384], P(None, ('row', 'col')), may hold values from -6 to 6
Outputs:
- test_basis: bfloat16 [5, 96, 16384], P(None, None, ('row', 'col'))
- triangular_factor: float32 [97, 97], replicated
- gauss_step: float32 [96], replicated
The draws below stay inside these ranges and needn't reach their ends.
Inputs may be any that keep to these rules, and one draw needn't show every extreme that they name: `face_cells`: the two cells of a face differ and lie at most 64 apart modulo 512. `ghost_counts`: entry 8 p + m counts the used slots of block m of partition p: from half of the block's size to all of it (32 for the first four blocks, 8 for the last four); in every draw some partition uses all slots of all its blocks.
All inputs are finite; a program needn't handle non-finite values. No bound on the sum of `limiter_flags` on one device may be relied on, other than what follows from the above.
Results may differ from the reference program's by a relative error of at most 0.0095.
Values may be sent and summed in bfloat16 or wider, within the bound.
A program may use at most 64 MiB of HBM per device.

```python
import math
import jax
import jax.numpy as jnp
import numpy as np
from jax import lax

F = 5
K = 96
CELLS_DEV = 512
FACE_CAP = 32
EDGE_CAP = 8
NCELLS = 16384
FACES = 32768
SLOTS_ALL = 5120
N_ROW = 8
N_COL = 4
DEVICES = 32


def draw_face_cells(key, part):
    left_cells = jax.random.randint(jax.random.fold_in(key, 11), (FACES,), 0, CELLS_DEV)
    stride_offset = jax.random.randint(jax.random.fold_in(key, 12), (FACES,), 1, 65)
    right_cells = (left_cells + stride_offset) % CELLS_DEV
    return jnp.stack([left_cells, right_cells]).astype(jnp.int32)


def draw_ghost_counts(key, part):
    capacity = jnp.tile(jnp.array([FACE_CAP] * 4 + [EDGE_CAP] * 4, jnp.int32), DEVICES)
    lowest_count = capacity // 2
    sampled = jax.random.randint(jax.random.fold_in(key, 21), (8 * DEVICES,), 0, 1 << 20)
    counts = lowest_count + sampled % (capacity - lowest_count + 1)
    chosen = jax.random.randint(jax.random.fold_in(key, 22), (), 0, DEVICES)
    owning_device = jnp.arange(8 * DEVICES, dtype=jnp.int32) // 8
    return jnp.where(owning_device == chosen, capacity, counts).astype(jnp.int32)


def touch_ends(entries, own_key, least, high):
    longest = entries.shape.index(max(entries.shape))
    spots = []
    for shift in (0, 1):
        where = [jax.random.randint(jax.random.fold_in(own_key, axis), (), 0, length) for axis, length in enumerate(entries.shape)]
        where[longest] = (where[longest] + shift) % entries.shape[longest]
        spots.append(tuple(where))
    return entries.at[spots[0]].set(least).at[spots[1]].set(high)


def levels(key, dims, shards, least, largest):
    def one(dim, shards_of):
        draws = jax.random.uniform(jax.random.fold_in(jax.random.fold_in(key, 6), dim), (shards_of,), jnp.float32, least / len(shards), largest / len(shards))
        return jnp.repeat(jnp.exp(draws), dims[dim] // shards_of).reshape((-1,) + (1,) * (len(dims) - dim - 1))

    gain = one(*shards[0])
    for cut in shards[1:]:
        gain = gain * one(*cut)
    return gain


def gaussian(stream_key, extent, width, most, pieces=(), kind=jnp.bfloat16):
    entries = width * jax.random.normal(stream_key, extent, jnp.float32)
    if pieces:
        entries = entries * levels(stream_key, extent, pieces, -0.22, 0.18)
    return jnp.clip(entries, -most, most).astype(kind)


def setup_inputs(seed: int = 0) -> dict:
    key_list = jax.random.split(jax.random.key(seed), 13)
    return {
        "reduced_basis": gaussian(key_list[0], (F, K, NCELLS), 1.0, 6.0, ((2, 32),)),
        "cell_jacobian": gaussian(key_list[1], (F, F, NCELLS), 0.5, 4.0, ((2, 32),), jnp.float32),
        "face_cells": draw_face_cells(jax.random.fold_in(key_list[12], 71), 0),
        "face_jacobian": gaussian(key_list[3], (2, F, F, FACES), 0.3, 3.0, ((3, 32),), jnp.float32),
        "limiter_flags": touch_ends((jax.random.randint(key_list[4], (FACES,), 0, 4) < 1).astype(jnp.int32), jax.random.fold_in(key_list[4], 1), 0, 1),
        "viscosity": jnp.clip(jnp.exp(jax.random.uniform(key_list[5], (F,), jnp.float32, math.log(0.1), math.log(1.0))), 0.1, 1.0),
        "ghost_cells": touch_ends(jax.random.randint(key_list[6], (SLOTS_ALL,), 0, CELLS_DEV), jax.random.fold_in(key_list[6], 1), 0, CELLS_DEV - 1).astype(jnp.int32),
        "ghost_jacobian": gaussian(key_list[7], (F, F, SLOTS_ALL), 0.3, 3.0, ((2, 32),), jnp.float32),
        "ghost_counts": draw_ghost_counts(jax.random.fold_in(key_list[12], 71), 0),
        "receive_cells": touch_ends(jax.random.randint(key_list[9], (SLOTS_ALL,), 0, CELLS_DEV), jax.random.fold_in(key_list[9], 1), 0, CELLS_DEV - 1).astype(jnp.int32),
        "coordinates": gaussian(key_list[10], (K,), 1.0, 5.0, (), jnp.float32),
        "base_residual": gaussian(key_list[11], (F, NCELLS), 1.0, 6.0, ((1, 32),), jnp.float32),
    }


direction_offsets = ((-1, 0), (1, 0), (0, -1), (0, 1), (-1, -1), (-1, 1), (1, -1), (1, 1))

def block_sizes():
    return [FACE_CAP] * 4 + [EDGE_CAP] * 4

def slot_limits(counts):
    capacity_each = block_sizes()
    slot_owner = np.concatenate([np.full(total_quantity, position, np.int32) for position, total_quantity in enumerate(capacity_each)])
    slot_position = np.concatenate([np.arange(total_quantity, dtype=np.int32) for total_quantity in capacity_each])
    compare = slot_owner[None, :] == np.arange(8, dtype=np.int32)[:, None]
    slot_limit = lax.optimization_barrier(jnp.sum(jnp.where(compare, counts[:, None], 0), axis=0))
    return slot_position < slot_limit

def upper_cholesky(matrix):
    order = matrix.shape[0]
    indices = jnp.arange(order, dtype=jnp.int32)

    def column_step(column, lower):
        row_vector = lax.dynamic_slice_in_dim(lower, column, 1, 0)[0]
        target = lax.dynamic_slice_in_dim(matrix, column, 1, 1)[:, 0]
        remain = target - jnp.dot(lower, row_vector, precision=lax.Precision.HIGHEST)
        pivot = jnp.sqrt(jnp.sum(jnp.where(indices == column, remain, 0.0)))
        new_column = jnp.where(indices > column, remain / pivot, jnp.where(indices == column, pivot, 0.0))
        return lax.dynamic_update_slice_in_dim(lower, new_column[:, None], column, 1)
    lower = lax.fori_loop(0, order, column_step, jnp.zeros_like(matrix))
    return lower.T

def upper_solve(upper, rhs):
    order = upper.shape[0]
    indices = jnp.arange(order, dtype=jnp.int32)

    def row_step(turn, solution):
        place = order - 1 - turn
        upper_row = lax.dynamic_slice_in_dim(upper, place, 1, 0)[0]
        known = jnp.dot(upper_row, solution, precision=lax.Precision.HIGHEST)
        pivot = jnp.sum(jnp.where(indices == place, upper_row, 0.0))
        target = jnp.sum(jnp.where(indices == place, rhs, 0.0))
        return jnp.where(indices == place, (target - known) / pivot, solution)
    return lax.fori_loop(0, order, row_step, jnp.zeros_like(rhs))

def per_device(array, devices):
    split_array = array.reshape(array.shape[:-1] + (devices, array.shape[-1] // devices))
    return jnp.moveaxis(split_array, -2, 0)

def ghost_partials(device_items):
    basis_block, ghost_block, jacobian_block, count_block = device_items
    gathered = jnp.take(basis_block, ghost_block, axis=2).astype(jnp.float32)
    partial_value = jnp.einsum('gfs,fks->gks', jacobian_block, gathered, precision=lax.Precision.HIGHEST)
    slot_kept = slot_limits(count_block)
    return jnp.where(slot_kept[None, None, :], partial_value, 0.0).astype(jnp.bfloat16)

def reference(reduced_basis, cell_jacobian, face_cells, face_jacobian, limiter_flags, viscosity, ghost_cells, ghost_jacobian, ghost_counts, receive_cells, coordinates, base_residual):
    devices = N_ROW * N_COL
    basis_dev = per_device(reduced_basis, devices)
    partials = lax.map(ghost_partials, (basis_dev, per_device(ghost_cells, devices), per_device(ghost_jacobian, devices), per_device(ghost_counts, devices)))
    partial_grid = partials.reshape((N_ROW, N_COL) + partials.shape[1:])
    padded = jnp.pad(partial_grid, ((1, 1), (1, 1), (0, 0), (0, 0), (0, 0)))
    fragment_list = []
    slot_start = 0
    for direction, offset_pair in enumerate(direction_offsets):
        row_offset, col_offset = offset_pair
        block_width = block_sizes()[direction]
        shifted = padded[1 - row_offset:1 - row_offset + N_ROW, 1 - col_offset:1 - col_offset + N_COL]
        fragment_list.append(shifted[..., slot_start:slot_start + block_width])
        slot_start += block_width
    incoming_block = jnp.concatenate(fragment_list, axis=-1).reshape(partials.shape)
    row_scale = (F * NCELLS) ** (-0.5)

    def device_work(device_items):
        basis_block, cell_tile_block, paired_block, face_block, flag_block, receive_block, got_block, base_block = device_items
        broad_basis_matrix = basis_block.astype(jnp.float32)
        jacobian_projection = jnp.einsum('irx,rtx->itx', cell_tile_block, broad_basis_matrix, precision=lax.Precision.HIGHEST)
        left_basis = jnp.take(broad_basis_matrix, paired_block[0], axis=2)
        right_basis = jnp.take(broad_basis_matrix, paired_block[1], axis=2)
        damping = viscosity[:, None, None] * flag_block.astype(jnp.float32)[None, None, :]
        difference = left_basis - right_basis
        to_left = jnp.einsum('gfn,fkn->gkn', face_block[0], right_basis, precision=lax.Precision.HIGHEST) + damping * difference
        to_right = jnp.einsum('gfn,fkn->gkn', face_block[1], left_basis, precision=lax.Precision.HIGHEST) - damping * difference
        jacobian_projection = jacobian_projection.at[:, :, paired_block[0]].add(to_left)
        jacobian_projection = jacobian_projection.at[:, :, paired_block[1]].add(to_right)
        jacobian_projection = jacobian_projection.at[:, :, receive_block].add(got_block.astype(jnp.float32))
        test_block = lax.optimization_barrier(jacobian_projection.astype(jnp.bfloat16))
        test_wide = test_block.astype(jnp.float32)
        residual_vector = base_block + row_scale * jnp.einsum('fkc,k->fc', test_wide, coordinates, precision=lax.Precision.HIGHEST)
        residual_low = lax.optimization_barrier(residual_vector.astype(jnp.bfloat16))
        stacked = jnp.concatenate([test_wide, residual_low.astype(jnp.float32)[:, None, :]], axis=1)
        gram_matrix = jnp.einsum('fkc,fjc->kj', stacked, stacked, precision=lax.Precision.HIGHEST) * (row_scale * row_scale)
        return (test_block, gram_matrix)
    test_blocks, gram_blocks = lax.map(device_work, (basis_dev, per_device(cell_jacobian, devices), per_device(face_cells, devices), per_device(face_jacobian, devices), per_device(limiter_flags, devices), per_device(receive_cells, devices), incoming_block, per_device(base_residual, devices)))
    test_basis = jnp.moveaxis(test_blocks, 0, 2).reshape(F, K, NCELLS)
    gram_sum = lax.optimization_barrier(jnp.sum(gram_blocks, axis=0))
    upper_factor = upper_cholesky(gram_sum)
    solved = upper_solve(upper_factor[:K, :K], upper_factor[:K, K])
    gauss_step = -solved / row_scale
    return (test_basis, upper_factor, gauss_step)
```

```python
import functools

import jax
import jax.numpy as jnp
from jax import lax
from jax.experimental import pallas as pl
from jax.experimental.pallas import tpu as pltpu
from jax.sharding import PartitionSpec as P

FACE_CAP = 32
EDGE_CAP = 8
EDGE_ROWS = 16
OFFSETS = ((-1, 0), (1, 0), (0, -1), (0, 1), (-1, -1), (-1, 1), (1, -1), (1, 1))
SLOTS = 4 * FACE_CAP + 4 * EDGE_CAP
SENT_ROWS = 4 * FACE_CAP + 4 * EDGE_ROWS
MESH = pl.DeviceIdType.MESH
BF16 = jnp.bfloat16
F32 = jnp.float32


def block_rows(m):
    if m < 4:
        return m * FACE_CAP, FACE_CAP
    return 4 * FACE_CAP + (m - 4) * EDGE_ROWS, EDGE_ROWS


def one_hot(cells, count):
    rows = lax.broadcasted_iota(jnp.int32, (count, cells.shape[1]), 0)
    return jnp.where(rows == cells, 1.0, 0.0).astype(BF16)


def matmul(a, b, dims):
    return lax.dot_general(a, b, (dims, ((), ())), preferred_element_type=F32)


def assemble(
    nrow, ncol, row_scale, tiles, chunk,
    basis, cellj, facec, facej, flags, visc, ghostc, ghostj, counts, recvc, coords, base,
    tb_out, gram_out,
    hot, terms, left_s, right_s, sent, got, stacked, gram_s, parts, mine, summed,
    halo_send, halo_recv, up_send, up_recv, down_send, down_recv,
):
    fields, modes, cells = basis.shape
    wide = fields * modes
    faces = facec.shape[1]
    devices = nrow * ncol
    row, col = lax.axis_index("row"), lax.axis_index("col")
    me = row * ncol + col

    def place(d):
        return (lax.div(d, jnp.int32(ncol)), lax.rem(d, jnp.int32(ncol)))

    barrier = pltpu.get_barrier_semaphore()

    @pl.loop(0, devices)
    def _(d):
        @pl.when(d != me)
        def _():
            pl.semaphore_signal(barrier, inc=1, device_id=place(d), device_id_type=MESH)

    flat = basis[...].reshape(wide, cells)

    slot = lax.broadcasted_iota(jnp.int32, (1, SLOTS), 1)
    limit = jnp.zeros((1, SLOTS), jnp.int32)
    start = 0
    for m in range(8):
        width = FACE_CAP if m < 4 else EDGE_CAP
        inside = (slot >= start) & (slot < start + width)
        limit = jnp.where(inside, counts[m] + start, limit)
        start += width
    kept = slot < limit
    ghosts = matmul(flat, one_hot(ghostc[...], cells), ((1,), (0,)))
    pieces = []
    for g in range(fields):
        total = None
        for f in range(fields):
            entry = jnp.where(kept, ghostj[g, f : f + 1, :], 0.0)
            term = entry * ghosts[f * modes : (f + 1) * modes]
            total = term if total is None else total + term
        pieces.append(total.astype(BF16))
    partial = jnp.concatenate(pieces, axis=0)
    lane = lax.broadcasted_iota(jnp.int32, (SENT_ROWS, SLOTS), 1)
    sub = lax.broadcasted_iota(jnp.int32, (SENT_ROWS, SLOTS), 0)
    edge = lane - 4 * FACE_CAP
    target = jnp.where(edge < 0, lane, lane + (edge >> 3) * (EDGE_ROWS - EDGE_CAP))
    spread = jnp.where(sub == target, 1.0, 0.0).astype(BF16)
    sent[...] = matmul(spread, partial, ((1,), (1,))).astype(BF16)
    placed = matmul(spread, one_hot(recvc[...], cells), ((1,), (1,))).astype(BF16)

    def inside_grid(dr, dc):
        ok = (row + dr >= 0) & (row + dr < nrow)
        return ok & (col + dc >= 0) & (col + dc < ncol)

    for m, (dr, dc) in enumerate(OFFSETS):
        first, count = block_rows(m)

        @pl.when(jnp.logical_not(inside_grid(-dr, -dc)))
        def _():
            got[first : first + count, :] = jnp.zeros((count, wide), BF16)

    pl.semaphore_wait(barrier, devices - 1)

    def halo(m):
        dr, dc = OFFSETS[m]
        first, count = block_rows(m)
        return pltpu.make_async_remote_copy(
            src_ref=sent.at[pl.ds(first, count)],
            dst_ref=got.at[pl.ds(first, count)],
            send_sem=halo_send.at[m],
            recv_sem=halo_recv.at[m],
            device_id=(row + dr, col + dc),
            device_id_type=MESH,
        )

    for m, (dr, dc) in enumerate(OFFSETS):
        @pl.when(inside_grid(dr, dc))
        def _():
            halo(m).start()

    @pl.loop(0, faces // chunk)
    def _(step):
        at = pl.multiple_of(step * chunk, chunk)
        span = pl.ds(at, chunk)
        span_b = pl.ds(pl.multiple_of(at + faces, chunk), chunk)
        pair = facec[:, span]
        hot_a = one_hot(pair[0:1], cells)
        hot_b = one_hot(pair[1:2], cells)
        hot[:, span] = hot_a
        hot[:, span_b] = hot_b
        left_s[...] = matmul(flat, hot_a, ((1,), (0,)))
        right_s[...] = matmul(flat, hot_b, ((1,), (0,)))
        flag = flags[:, span].astype(F32)
        mark = jnp.where(
            lax.broadcasted_iota(jnp.int32, (16, chunk), 0) == 0, flag, 0.0
        ).astype(BF16)
        for side, values, where_to in ((0, right_s, span), (1, left_s, span_b)):
            jac = facej[side, :, :, span]
            for g in range(fields):
                total = None
                for f in range(fields):
                    entry = jac[g, f : f + 1, :]
                    if f == g:
                        entry = entry - visc[g] * flag
                    term = entry * values[f * modes : (f + 1) * modes, :]
                    total = term if total is None else total + term
                terms[g * modes : (g + 1) * modes, where_to] = total.astype(BF16)
            terms[wide : wide + 16, where_to] = mark

    image = matmul(terms[...], hot[...], ((1,), (1,)))
    flagged = image[wide : wide + 1, :]
    rows = []
    for g in range(fields):
        total = image[g * modes : (g + 1) * modes, :]
        for f in range(fields):
            entry = cellj[g, f : f + 1, :]
            if f == g:
                entry = entry + visc[g] * flagged
            total = total + entry * basis[f].astype(F32)
        rows.append(total)

    for m, (dr, dc) in enumerate(OFFSETS):
        @pl.when(inside_grid(-dr, -dc))
        def _():
            halo(m).wait_recv()

    arrived = matmul(got[...], placed, ((0,), (0,)))
    c = coords[...]
    high = c.astype(BF16).astype(F32)
    mid = (c - high).astype(BF16).astype(F32)
    low = c - high - mid
    sub16 = lax.broadcasted_iota(jnp.int32, (16, modes), 0)
    weights = jnp.where(
        sub16 == 0, high, jnp.where(sub16 == 1, mid, jnp.where(sub16 == 2, low, 0.0))
    ).astype(BF16)
    top = lax.broadcasted_iota(jnp.int32, (16, cells), 0) == 0
    gram = None
    for g in range(fields):
        basis_g = (rows[g] + arrived[g * modes : (g + 1) * modes]).astype(BF16)
        tb_out[g] = basis_g
        stacked[g, :modes, :] = basis_g
        shift = jnp.sum(matmul(weights, basis_g, ((1,), (0,))), axis=0, keepdims=True)
        resid = base[g : g + 1, :] + row_scale * shift
        stacked[g, modes : modes + 16, :] = jnp.where(top, resid, 0.0).astype(BF16)
        stacked[g, modes + 16 :, :] = jnp.zeros((128 - modes - 16, cells), BF16)
        x = stacked[g]
        part = matmul(x, x, ((1,), (1,)))
        gram = part if gram is None else gram + part
    gram_s[...] = gram[: tiles * 8].reshape(tiles, 8, 128)

    def owner(t):
        return (t * devices) // tiles

    my_tile = lax.div(me * tiles + (devices - 1), jnp.int32(devices))
    tile = jnp.minimum(my_tile, tiles - 1)
    owns = (my_tile < tiles) & (lax.div(tile * devices, jnp.int32(tiles)) == me)

    def up(t):
        o = owner(t)
        return pltpu.make_async_remote_copy(
            src_ref=gram_s.at[t],
            dst_ref=parts.at[me],
            send_sem=up_send.at[t],
            recv_sem=up_recv.at[me],
            device_id=(jnp.int32(o // ncol), jnp.int32(o % ncol)),
            device_id_type=MESH,
        )

    for t in range(tiles):
        @pl.when(me != owner(t))
        def _():
            up(t).start()

        @pl.when(me == owner(t))
        def _():
            parts[me] = gram_s[t]

    def down(d):
        return pltpu.make_async_remote_copy(
            src_ref=mine,
            dst_ref=summed.at[tile],
            send_sem=down_send.at[d],
            recv_sem=down_recv.at[tile],
            device_id=place(d),
            device_id_type=MESH,
        )

    @pl.when(owns)
    def _():
        @pl.loop(0, devices)
        def _(d):
            @pl.when(d != me)
            def _():
                pltpu.make_async_remote_copy(
                    src_ref=mine,
                    dst_ref=parts.at[d],
                    send_sem=down_send.at[d],
                    recv_sem=up_recv.at[d],
                    device_id=place(d),
                    device_id_type=MESH,
                ).wait_recv()

        total = jnp.sum(parts[...], axis=0)
        mine[...] = total
        summed[tile] = total

        @pl.loop(0, devices)
        def _(d):
            @pl.when(d != me)
            def _():
                down(d).start()

    for t in range(tiles):
        @pl.when(me != owner(t))
        def _():
            pltpu.make_async_remote_copy(
                src_ref=mine,
                dst_ref=summed.at[t],
                send_sem=up_send.at[t],
                recv_sem=down_recv.at[t],
                device_id=place(jnp.int32(owner(t))),
                device_id_type=MESH,
            ).wait_recv()

    gram_out[...] = summed[...]

    for m, (dr, dc) in enumerate(OFFSETS):
        @pl.when(inside_grid(dr, dc))
        def _():
            halo(m).wait_send()

    for t in range(tiles):
        @pl.when(me != owner(t))
        def _():
            up(t).wait_send()

    @pl.when(owns)
    def _():
        @pl.loop(0, devices)
        def _(d):
            @pl.when(d != me)
            def _():
                down(d).wait_send()


def factor(modes, row_scale, gram, tb_in, upper, step, tb_out, sem):
    passing = pltpu.make_async_copy(tb_in, tb_out, sem)
    passing.start()
    tiles = gram.shape[0]
    order = modes + 1
    shape = (8, 128)
    sub = lax.broadcasted_iota(jnp.int32, shape, 0)
    lane = lax.broadcasted_iota(jnp.int32, shape, 1)

    def across(x, s):
        return jnp.broadcast_to(x[s : s + 1, :], shape)

    rows = [gram[t] * (row_scale * row_scale) for t in range(tiles)]
    done = [jnp.zeros(shape, F32) for _ in range(tiles)]
    for p in range(tiles):
        columns = range(8 * p, min(8 * p + 8, order))
        held = {
            j: [jnp.broadcast_to(rows[t][:, j : j + 1], shape) for t in range(tiles)]
            for j in columns
        }
        for j in columns:
            s = j % 8
            here = sub == s
            inverse = lax.rsqrt(across(held[j][p], s))
            pivot_row = across(rows[p], s) * inverse
            done[p] = jnp.where(here, pivot_row, done[p])
            if j == modes:
                break
            scaled = [x * inverse for x in held[j]]
            for t in range(tiles):
                new = rows[t] - scaled[t] * pivot_row
                rows[t] = jnp.where(here, pivot_row * inverse, new) if t == p else new
            for i in columns:
                if i <= j:
                    continue
                entry = across(scaled[p], i % 8)
                for t in range(tiles):
                    new = held[i][t] - scaled[t] * entry
                    held[i][t] = jnp.where(here, entry * inverse, new) if t == p else new
    solved = jnp.zeros(shape, F32)
    for t in range(tiles):
        kept = jnp.where(lane >= sub + 8 * t, done[t], 0.0)
        count = min(8, order - 8 * t)
        upper[8 * t : 8 * t + count, :] = kept[:count, :order]
        if 8 * t < modes:
            last = jnp.broadcast_to(rows[t][:, modes : modes + 1], shape)
            solved = solved + jnp.where(lane == sub + 8 * t, last, 0.0)
    step[...] = (jnp.sum(solved, axis=0, keepdims=True) * (-1.0 / row_scale))[:, :modes]
    passing.wait()


def local(
    nrow, ncol,
    reduced_basis, cell_jacobian, face_cells, face_jacobian, limiter_flags, viscosity,
    ghost_cells, ghost_jacobian, ghost_counts, receive_cells, coordinates, base_residual,
):
    fields, modes, cells = reduced_basis.shape
    faces = face_cells.shape[1]
    devices = nrow * ncol
    wide = fields * modes
    row_scale = float((fields * cells * devices) ** (-0.5))
    tiles = (modes + 1 + 7) // 8
    chunk = 256
    vmem = pl.BlockSpec(memory_space=pltpu.VMEM)
    smem = pl.BlockSpec(memory_space=pltpu.SMEM)
    dma = pltpu.SemaphoreType.DMA
    test_basis, gram = pl.pallas_call(
        functools.partial(assemble, nrow, ncol, row_scale, tiles, chunk),
        out_shape=(
            jax.ShapeDtypeStruct((fields, modes, cells), BF16),
            jax.ShapeDtypeStruct((tiles, 8, 128), F32),
        ),
        in_specs=[vmem, vmem, vmem, vmem, vmem, smem, vmem, vmem, smem, vmem, vmem, vmem],
        out_specs=(vmem, vmem),
        scratch_shapes=[
            pltpu.VMEM((cells, 2 * faces), BF16),
            pltpu.VMEM((wide + 16, 2 * faces), BF16),
            pltpu.VMEM((wide, chunk), F32),
            pltpu.VMEM((wide, chunk), F32),
            pltpu.VMEM((SENT_ROWS, wide), BF16),
            pltpu.VMEM((SENT_ROWS, wide), BF16),
            pltpu.VMEM((fields, 128, cells), BF16),
            pltpu.VMEM((tiles, 8, 128), F32),
            pltpu.VMEM((devices, 8, 128), F32),
            pltpu.VMEM((8, 128), F32),
            pltpu.VMEM((tiles, 8, 128), F32),
            dma((8,)), dma((8,)), dma((tiles,)), dma((devices,)), dma((devices,)), dma((tiles,)),
        ],
        compiler_params=pltpu.CompilerParams(
            collective_id=0, has_side_effects=True, vmem_limit_bytes=48 * 1024 * 1024
        ),
        cost_estimate=pl.CostEstimate(
            flops=8 * wide * cells * faces, bytes_accessed=3_000_000, transcendentals=0
        ),
        name="assemble",
    )(
        reduced_basis, cell_jacobian, face_cells, face_jacobian, limiter_flags.reshape(1, -1),
        viscosity, ghost_cells.reshape(1, -1), ghost_jacobian, ghost_counts,
        receive_cells.reshape(1, -1), coordinates.reshape(1, -1), base_residual,
    )
    upper, step, test_basis = pl.pallas_call(
        functools.partial(factor, modes, row_scale),
        out_shape=(
            jax.ShapeDtypeStruct((modes + 1, modes + 1), F32),
            jax.ShapeDtypeStruct((1, modes), F32),
            jax.ShapeDtypeStruct((fields, modes, cells), BF16),
        ),
        in_specs=[vmem, pl.BlockSpec(memory_space=pl.ANY)],
        out_specs=(vmem, vmem, pl.BlockSpec(memory_space=pl.ANY)),
        scratch_shapes=[pltpu.SemaphoreType.DMA],
        name="factor",
    )(gram, test_basis)
    return test_basis, upper, step.reshape(modes)


def solution(mesh):
    both = ("row", "col")
    placed = (
        P(None, None, both), P(None, None, both), P(None, both), P(None, None, None, both),
        P(both), P(), P(both), P(None, None, both), P(both), P(both), P(), P(None, both),
    )
    return jax.shard_map(
        functools.partial(local, mesh.shape["row"], mesh.shape["col"]),
        mesh=mesh,
        in_specs=placed,
        out_specs=(P(None, None, both), P(), P()),
        check_vma=False,
    )
```

```python
import functools

import jax
import jax.numpy as jnp
from jax import lax
from jax.experimental import pallas as pl
from jax.experimental.pallas import tpu as pltpu
from jax.sharding import PartitionSpec as P

FACE_CAP = 32
EDGE_CAP = 8
EDGE_ROWS = 16
OFFSETS = ((-1, 0), (1, 0), (0, -1), (0, 1), (-1, -1), (-1, 1), (1, -1), (1, 1))
SLOTS = 4 * FACE_CAP + 4 * EDGE_CAP
SENT_ROWS = 4 * FACE_CAP + 4 * EDGE_ROWS
MESH = pl.DeviceIdType.MESH
BF16 = jnp.bfloat16
F32 = jnp.float32


def block_rows(m):
    if m < 4:
        return m * FACE_CAP, FACE_CAP
    return 4 * FACE_CAP + (m - 4) * EDGE_ROWS, EDGE_ROWS


def one_hot(cells, count):
    rows = lax.broadcasted_iota(jnp.int32, (count, cells.shape[1]), 0)
    return jnp.where(rows == cells, 1.0, 0.0).astype(BF16)


def matmul(a, b, dims):
    return lax.dot_general(a, b, (dims, ((), ())), preferred_element_type=F32)


def assemble(
    nrow, ncol, row_scale, tiles, chunk,
    basis_h, cellj_h, facec_h, facej_h, flags_h, visc_h, ghostc_h, ghostj_h, counts_h, recvc_h,
    coords_h, base_h,
    tb_out, gram_out,
    basis, cellj, facec, facej, flags, visc, ghostc, ghostj, counts, recvc, coords, base, in_sem,
    tb_sem, hot, terms, left_s, right_s, sent, got, stacked, gram_s, parts, mine, summed,
    halo_send, halo_recv, up_send, up_recv, down_send, down_recv,
):
    fields, modes, cells = basis.shape
    wide = fields * modes
    faces = facec.shape[1]
    devices = nrow * ncol
    row, col = lax.axis_index("row"), lax.axis_index("col")
    me = row * ncol + col

    def place(d):
        return (lax.div(d, jnp.int32(ncol)), lax.rem(d, jnp.int32(ncol)))

    names = ("basis", "ghostc", "counts", "ghostj", "recvc", "facec", "flags", "visc", "facej",
             "cellj", "coords", "base")
    inputs = dict(
        basis=(basis_h, basis), ghostc=(ghostc_h, ghostc), counts=(counts_h, counts),
        ghostj=(ghostj_h, ghostj), recvc=(recvc_h, recvc), facec=(facec_h, facec),
        flags=(flags_h, flags), visc=(visc_h, visc), facej=(facej_h, facej),
        cellj=(cellj_h, cellj), coords=(coords_h, coords), base=(base_h, base),
    )

    def fetch(name):
        return pltpu.make_async_copy(*inputs[name], in_sem.at[names.index(name)])

    for name in names:
        fetch(name).start()

    barrier = pltpu.get_barrier_semaphore()

    @pl.loop(0, devices)
    def _(d):
        @pl.when(d != me)
        def _():
            pl.semaphore_signal(barrier, inc=1, device_id=place(d), device_id_type=MESH)

    for name in names[:5]:
        fetch(name).wait()
    flat = basis[...].reshape(wide, cells)

    slot = lax.broadcasted_iota(jnp.int32, (1, SLOTS), 1)
    limit = jnp.zeros((1, SLOTS), jnp.int32)
    start = 0
    for m in range(8):
        width = FACE_CAP if m < 4 else EDGE_CAP
        inside = (slot >= start) & (slot < start + width)
        limit = jnp.where(inside, counts[m] + start, limit)
        start += width
    kept = slot < limit
    ghosts = matmul(flat, one_hot(ghostc[...], cells), ((1,), (0,)))
    pieces = []
    for g in range(fields):
        total = None
        for f in range(fields):
            entry = jnp.where(kept, ghostj[g, f : f + 1, :], 0.0)
            term = entry * ghosts[f * modes : (f + 1) * modes]
            total = term if total is None else total + term
        pieces.append(total.astype(BF16))
    partial = jnp.concatenate(pieces, axis=0)
    lane = lax.broadcasted_iota(jnp.int32, (SENT_ROWS, SLOTS), 1)
    sub = lax.broadcasted_iota(jnp.int32, (SENT_ROWS, SLOTS), 0)
    edge = lane - 4 * FACE_CAP
    target = jnp.where(edge < 0, lane, lane + (edge >> 3) * (EDGE_ROWS - EDGE_CAP))
    spread = jnp.where(sub == target, 1.0, 0.0).astype(BF16)
    sent[...] = matmul(spread, partial, ((1,), (1,))).astype(BF16)
    placed = matmul(spread, one_hot(recvc[...], cells), ((1,), (1,))).astype(BF16)

    def inside_grid(dr, dc):
        ok = (row + dr >= 0) & (row + dr < nrow)
        return ok & (col + dc >= 0) & (col + dc < ncol)

    for m, (dr, dc) in enumerate(OFFSETS):
        first, count = block_rows(m)

        @pl.when(jnp.logical_not(inside_grid(-dr, -dc)))
        def _():
            got[first : first + count, :] = jnp.zeros((count, wide), BF16)

    pl.semaphore_wait(barrier, devices - 1)

    def halo(m):
        dr, dc = OFFSETS[m]
        first, count = block_rows(m)
        return pltpu.make_async_remote_copy(
            src_ref=sent.at[pl.ds(first, count)],
            dst_ref=got.at[pl.ds(first, count)],
            send_sem=halo_send.at[m],
            recv_sem=halo_recv.at[m],
            device_id=(row + dr, col + dc),
            device_id_type=MESH,
        )

    for m, (dr, dc) in enumerate(OFFSETS):
        @pl.when(inside_grid(dr, dc))
        def _():
            halo(m).start()

    for name in names[5:9]:
        fetch(name).wait()

    @pl.loop(0, faces // chunk)
    def _(step):
        at = pl.multiple_of(step * chunk, chunk)
        span = pl.ds(at, chunk)
        span_b = pl.ds(pl.multiple_of(at + faces, chunk), chunk)
        pair = facec[:, span]
        hot_a = one_hot(pair[0:1], cells)
        hot_b = one_hot(pair[1:2], cells)
        hot[:, span] = hot_a
        hot[:, span_b] = hot_b
        left_s[...] = matmul(flat, hot_a, ((1,), (0,)))
        right_s[...] = matmul(flat, hot_b, ((1,), (0,)))
        flag = flags[:, span].astype(F32)
        mark = jnp.where(
            lax.broadcasted_iota(jnp.int32, (16, chunk), 0) == 0, flag, 0.0
        ).astype(BF16)
        for side, values, where_to in ((0, right_s, span), (1, left_s, span_b)):
            for g in range(fields):
                total = None
                for f in range(fields):
                    entry = facej[g, f, side : side + 1, span]
                    if f == g:
                        entry = entry - visc[g] * flag
                    term = entry * values[f * modes : (f + 1) * modes, :]
                    total = term if total is None else total + term
                terms[g * modes : (g + 1) * modes, where_to] = total.astype(BF16)
            terms[wide : wide + 16, where_to] = mark

    image = matmul(terms[...], hot[...], ((1,), (1,)))
    for name in names[9:]:
        fetch(name).wait()
    flagged = image[wide : wide + 1, :]
    rows = []
    for g in range(fields):
        total = image[g * modes : (g + 1) * modes, :]
        for f in range(fields):
            entry = cellj[g, f : f + 1, :]
            if f == g:
                entry = entry + visc[g] * flagged
            total = total + entry * basis[f].astype(F32)
        rows.append(total)

    for m, (dr, dc) in enumerate(OFFSETS):
        @pl.when(inside_grid(-dr, -dc))
        def _():
            halo(m).wait_recv()

    arrived = matmul(got[...], placed, ((0,), (0,)))
    c = coords[...]
    high = c.astype(BF16).astype(F32)
    mid = (c - high).astype(BF16).astype(F32)
    low = c - high - mid
    sub16 = lax.broadcasted_iota(jnp.int32, (16, modes), 0)
    weights = jnp.where(
        sub16 == 0, high, jnp.where(sub16 == 1, mid, jnp.where(sub16 == 2, low, 0.0))
    ).astype(BF16)
    top = lax.broadcasted_iota(jnp.int32, (16, cells), 0) == 0
    gram = None

    def give(g):
        return pltpu.make_async_copy(
            stacked.at[g, pl.ds(0, modes)], tb_out.at[g], tb_sem.at[g]
        )

    for g in range(fields):
        basis_g = (rows[g] + arrived[g * modes : (g + 1) * modes]).astype(BF16)
        stacked[g, :modes, :] = basis_g
        give(g).start()
        shift = jnp.sum(matmul(weights, basis_g, ((1,), (0,))), axis=0, keepdims=True)
        resid = base[g : g + 1, :] + row_scale * shift
        stacked[g, modes : modes + 16, :] = jnp.where(top, resid, 0.0).astype(BF16)
        stacked[g, modes + 16 :, :] = jnp.zeros((128 - modes - 16, cells), BF16)
        x = stacked[g]
        part = matmul(x, x, ((1,), (1,)))
        gram = part if gram is None else gram + part
    gram_s[...] = gram[: tiles * 8].reshape(tiles, 8, 128)

    def owner(t):
        return (t * devices) // tiles

    my_tile = lax.div(me * tiles + (devices - 1), jnp.int32(devices))
    tile = jnp.minimum(my_tile, tiles - 1)
    owns = (my_tile < tiles) & (lax.div(tile * devices, jnp.int32(tiles)) == me)

    def up(t):
        o = owner(t)
        return pltpu.make_async_remote_copy(
            src_ref=gram_s.at[t],
            dst_ref=parts.at[me],
            send_sem=up_send.at[t],
            recv_sem=up_recv.at[me],
            device_id=(jnp.int32(o // ncol), jnp.int32(o % ncol)),
            device_id_type=MESH,
        )

    for t in range(tiles):
        @pl.when(me != owner(t))
        def _():
            up(t).start()

        @pl.when(me == owner(t))
        def _():
            parts[me] = gram_s[t]

    def down(d):
        return pltpu.make_async_remote_copy(
            src_ref=mine,
            dst_ref=summed.at[tile],
            send_sem=down_send.at[d],
            recv_sem=down_recv.at[tile],
            device_id=place(d),
            device_id_type=MESH,
        )

    @pl.when(owns)
    def _():
        @pl.loop(0, devices)
        def _(d):
            @pl.when(d != me)
            def _():
                pltpu.make_async_remote_copy(
                    src_ref=mine,
                    dst_ref=parts.at[d],
                    send_sem=down_send.at[d],
                    recv_sem=up_recv.at[d],
                    device_id=place(d),
                    device_id_type=MESH,
                ).wait_recv()

        total = jnp.sum(parts[...], axis=0)
        mine[...] = total
        summed[tile] = total

        @pl.loop(0, devices)
        def _(d):
            @pl.when(d != me)
            def _():
                down(d).start()

    for t in range(tiles):
        @pl.when(me != owner(t))
        def _():
            pltpu.make_async_remote_copy(
                src_ref=mine,
                dst_ref=summed.at[t],
                send_sem=up_send.at[t],
                recv_sem=down_recv.at[t],
                device_id=place(jnp.int32(owner(t))),
                device_id_type=MESH,
            ).wait_recv()

    gram_out[...] = summed[...]

    for g in range(fields):
        give(g).wait()

    for m, (dr, dc) in enumerate(OFFSETS):
        @pl.when(inside_grid(dr, dc))
        def _():
            halo(m).wait_send()

    for t in range(tiles):
        @pl.when(me != owner(t))
        def _():
            up(t).wait_send()

    @pl.when(owns)
    def _():
        @pl.loop(0, devices)
        def _(d):
            @pl.when(d != me)
            def _():
                down(d).wait_send()


def factor(modes, row_scale, gram, tb_in, upper, step, tb_out, sem):
    passing = pltpu.make_async_copy(tb_in, tb_out, sem)
    passing.start()
    tiles = gram.shape[0]
    order = modes + 1
    shape = (8, 128)
    sub = lax.broadcasted_iota(jnp.int32, shape, 0)
    lane = lax.broadcasted_iota(jnp.int32, shape, 1)

    def across(x, s):
        return jnp.broadcast_to(x[s : s + 1, :], shape)

    def along(x, c):
        return jnp.broadcast_to(x[:, c : c + 1], shape)

    rows = [gram[t] * (row_scale * row_scale) for t in range(tiles)]
    done = []
    for p in range(tiles):
        count = min(8, order - 8 * p)
        line = [across(rows[p], i) for i in range(count)]
        entry = {
            (i, k): along(line[i], 8 * p + k) for i in range(count) for k in range(i, count)
        }
        last = p == tiles - 1
        column = {
            t: [along(rows[t], 8 * p + j) for j in range(count)]
            for t in range(tiles) if t != p and not last
        }
        ahead = list(column[p + 1]) if not last else []
        factored, inverse, scaled = [], [], []
        for j in range(count):
            root = lax.rsqrt(entry[j, j])
            inverse.append(root * root)
            factored.append(line[j] * root)
            scaled.append(line[j] * inverse[j])
            for i in range(j + 1, count):
                ratio = entry[j, i] * inverse[j]
                for k in range(i, count):
                    entry[i, k] = entry[i, k] - ratio * entry[j, k]
                line[i] = line[i] - ratio * line[j]
                ahead[i] = ahead[i] - ratio * ahead[j]
        tile = factored[0]
        for j in range(1, count):
            tile = jnp.where(sub == j, factored[j], tile)
        done.append(tile)
        if last:
            break
        new = rows[p + 1]
        for j in range(count):
            new = new - ahead[j] * scaled[j]
        rows[p + 1] = new
        reduced = list(scaled)
        for j in range(count - 1, -1, -1):
            for k in range(j + 1, count):
                reduced[j] = reduced[j] - entry[j, k] * inverse[j] * reduced[k]
        for t in range(tiles):
            if t == p or t == p + 1:
                continue
            new = rows[t]
            for j in range(count):
                new = new - column[t][j] * reduced[j]
            rows[t] = new
        tile = reduced[0]
        for j in range(1, count):
            tile = jnp.where(sub == j, reduced[j], tile)
        rows[p] = tile
    solved = jnp.zeros(shape, F32)
    for t in range(tiles):
        kept = jnp.where(lane >= sub + 8 * t, done[t], 0.0)
        count = min(8, order - 8 * t)
        upper[8 * t : 8 * t + count, :] = kept[:count, :order]
        if 8 * t < modes:
            tail = along(rows[t], modes)
            solved = solved + jnp.where(lane == sub + 8 * t, tail, 0.0)
    step[...] = (jnp.sum(solved, axis=0, keepdims=True) * (-1.0 / row_scale))[:, :modes]
    passing.wait()


def local(
    nrow, ncol,
    reduced_basis, cell_jacobian, face_cells, face_jacobian, limiter_flags, viscosity,
    ghost_cells, ghost_jacobian, ghost_counts, receive_cells, coordinates, base_residual,
):
    fields, modes, cells = reduced_basis.shape
    faces = face_cells.shape[1]
    devices = nrow * ncol
    wide = fields * modes
    row_scale = float((fields * cells * devices) ** (-0.5))
    tiles = (modes + 1 + 7) // 8
    chunk = 256
    vmem = pl.BlockSpec(memory_space=pltpu.VMEM)
    hbm = pl.BlockSpec(memory_space=pltpu.HBM)
    dma = pltpu.SemaphoreType.DMA
    test_basis, gram = pl.pallas_call(
        functools.partial(assemble, nrow, ncol, row_scale, tiles, chunk),
        out_shape=(
            jax.ShapeDtypeStruct((fields, modes, cells), BF16),
            jax.ShapeDtypeStruct((tiles, 8, 128), F32),
        ),
        in_specs=[hbm] * 12,
        out_specs=(hbm, vmem),
        scratch_shapes=[
            pltpu.VMEM((fields, modes, cells), BF16),
            pltpu.VMEM((fields, fields, cells), F32),
            pltpu.VMEM((2, faces), jnp.int32),
            pltpu.VMEM((fields, fields, 2, faces), F32),
            pltpu.VMEM((1, faces), jnp.int32),
            pltpu.SMEM((fields,), F32),
            pltpu.VMEM((1, SLOTS), jnp.int32),
            pltpu.VMEM((fields, fields, SLOTS), F32),
            pltpu.SMEM((8,), jnp.int32),
            pltpu.VMEM((1, SLOTS), jnp.int32),
            pltpu.VMEM((1, modes), F32),
            pltpu.VMEM((fields, cells), F32),
            dma((12,)),
            dma((fields,)),
            pltpu.VMEM((cells, 2 * faces), BF16),
            pltpu.VMEM((wide + 16, 2 * faces), BF16),
            pltpu.VMEM((wide, chunk), F32),
            pltpu.VMEM((wide, chunk), F32),
            pltpu.VMEM((SENT_ROWS, wide), BF16),
            pltpu.VMEM((SENT_ROWS, wide), BF16),
            pltpu.VMEM((fields, 128, cells), BF16),
            pltpu.VMEM((tiles, 8, 128), F32),
            pltpu.VMEM((devices, 8, 128), F32),
            pltpu.VMEM((8, 128), F32),
            pltpu.VMEM((tiles, 8, 128), F32),
            dma((8,)), dma((8,)), dma((tiles,)), dma((devices,)), dma((devices,)), dma((tiles,)),
        ],
        compiler_params=pltpu.CompilerParams(
            collective_id=0, has_side_effects=True, vmem_limit_bytes=64 * 1024 * 1024 - 65536
        ),
        cost_estimate=pl.CostEstimate(
            flops=8 * wide * cells * faces, bytes_accessed=3_000_000, transcendentals=0
        ),
        name="assemble",
    )(
        reduced_basis, cell_jacobian, face_cells, face_jacobian.transpose(1, 2, 0, 3),
        limiter_flags.reshape(1, -1),
        viscosity, ghost_cells.reshape(1, -1), ghost_jacobian, ghost_counts,
        receive_cells.reshape(1, -1), coordinates.reshape(1, -1), base_residual,
    )
    upper, step, test_basis = pl.pallas_call(
        functools.partial(factor, modes, row_scale),
        out_shape=(
            jax.ShapeDtypeStruct((modes + 1, modes + 1), F32),
            jax.ShapeDtypeStruct((1, modes), F32),
            jax.ShapeDtypeStruct((fields, modes, cells), BF16),
        ),
        in_specs=[vmem, hbm],
        out_specs=(vmem, vmem, hbm),
        scratch_shapes=[pltpu.SemaphoreType.DMA],
        compiler_params=pltpu.CompilerParams(vmem_limit_bytes=64 * 1024 * 1024 - 65536),
        name="factor",
    )(gram, test_basis)
    return test_basis, upper, step.reshape(modes)


def solution(mesh):
    both = ("row", "col")
    placed = (
        P(None, None, both), P(None, None, both), P(None, both), P(None, None, None, both),
        P(both), P(), P(both), P(None, None, both), P(both), P(both), P(), P(None, both),
    )
    return jax.shard_map(
        functools.partial(local, mesh.shape["row"], mesh.shape["col"]),
        mesh=mesh,
        in_specs=placed,
        out_specs=(P(None, None, both), P(), P()),
        check_vma=False,
    )
```

```python
import functools

import jax
import jax.numpy as jnp
from jax import lax
from jax.experimental import pallas as pl
from jax.experimental.pallas import tpu as pltpu
from jax.sharding import PartitionSpec as P

FACE_CAP = 32
EDGE_CAP = 8
EDGE_ROWS = 16
OFFSETS = ((-1, 0), (1, 0), (0, -1), (0, 1), (-1, -1), (-1, 1), (1, -1), (1, 1))
SLOTS = 4 * FACE_CAP + 4 * EDGE_CAP
SENT_ROWS = 4 * FACE_CAP + 4 * EDGE_ROWS
MESH = pl.DeviceIdType.MESH
BF16 = jnp.bfloat16
F32 = jnp.float32


def block_rows(m):
    if m < 4:
        return m * FACE_CAP, FACE_CAP
    return 4 * FACE_CAP + (m - 4) * EDGE_ROWS, EDGE_ROWS


def one_hot(cells, count):
    rows = lax.broadcasted_iota(jnp.int32, (count, cells.shape[1]), 0)
    return jnp.where(rows == cells, 1.0, 0.0).astype(BF16)


def matmul(a, b, dims):
    return lax.dot_general(a, b, (dims, ((), ())), preferred_element_type=F32)


def assemble(
    nrow, ncol, row_scale, last_tile, tiles, chunk,
    basis_h, cellj_h, facec_h, facej_h, flags_h, visc_h, ghostc_h, ghostj_h, counts_h, recvc_h,
    coords_h, base_h,
    tb_out, gram_out,
    basis, cellj, facec, facej, flags, visc, ghostc, ghostj, counts, recvc, coords, base, in_sem,
    tb_sem, hot, terms, left_s, right_s, sent, got, stacked, gram_s, parts, mine, summed,
    halo_send, halo_recv, up_send, up_recv, down_send, down_recv,
):
    fields, modes, cells = basis.shape
    wide = fields * modes
    faces = facec.shape[1]
    devices = nrow * ncol
    row, col = lax.axis_index("row"), lax.axis_index("col")
    me = row * ncol + col

    def place(d):
        return (lax.div(d, jnp.int32(ncol)), lax.rem(d, jnp.int32(ncol)))

    names = ("basis", "ghostc", "counts", "ghostj", "recvc", "facec", "flags", "visc", "facej",
             "cellj", "coords", "base")
    inputs = dict(
        basis=(basis_h, basis), ghostc=(ghostc_h, ghostc), counts=(counts_h, counts),
        ghostj=(ghostj_h, ghostj), recvc=(recvc_h, recvc), facec=(facec_h, facec),
        flags=(flags_h, flags), visc=(visc_h, visc), facej=(facej_h, facej),
        cellj=(cellj_h, cellj), coords=(coords_h, coords), base=(base_h, base),
    )

    def fetch(name):
        return pltpu.make_async_copy(*inputs[name], in_sem.at[names.index(name)])

    for name in names:
        fetch(name).start()

    barrier = pltpu.get_barrier_semaphore()

    others = [lax.rem(me + k, jnp.int32(devices)) for k in range(1, devices)]
    for d in others:
        pl.semaphore_signal(barrier, inc=1, device_id=place(d), device_id_type=MESH)

    for name in names[:5]:
        fetch(name).wait()
    flat = basis[...].reshape(wide, cells)

    slot = lax.broadcasted_iota(jnp.int32, (1, SLOTS), 1)
    limit = jnp.zeros((1, SLOTS), jnp.int32)
    start = 0
    for m in range(8):
        width = FACE_CAP if m < 4 else EDGE_CAP
        inside = (slot >= start) & (slot < start + width)
        limit = jnp.where(inside, counts[m] + start, limit)
        start += width
    kept = slot < limit
    ghosts = matmul(flat, one_hot(ghostc[...], cells), ((1,), (0,)))
    pieces = []
    for g in range(fields):
        total = None
        for f in range(fields):
            entry = jnp.where(kept, ghostj[g, f : f + 1, :], 0.0)
            term = entry * ghosts[f * modes : (f + 1) * modes]
            total = term if total is None else total + term
        pieces.append(total.astype(BF16))
    partial = jnp.concatenate(pieces, axis=0)
    lane = lax.broadcasted_iota(jnp.int32, (SENT_ROWS, SLOTS), 1)
    sub = lax.broadcasted_iota(jnp.int32, (SENT_ROWS, SLOTS), 0)
    edge = lane - 4 * FACE_CAP
    target = jnp.where(edge < 0, lane, lane + (edge >> 3) * (EDGE_ROWS - EDGE_CAP))
    spread = jnp.where(sub == target, 1.0, 0.0).astype(BF16)
    sent[...] = matmul(spread, partial, ((1,), (1,))).astype(BF16)

    def inside_grid(dr, dc):
        ok = (row + dr >= 0) & (row + dr < nrow)
        return ok & (col + dc >= 0) & (col + dc < ncol)

    for m, (dr, dc) in enumerate(OFFSETS):
        first, count = block_rows(m)

        @pl.when(jnp.logical_not(inside_grid(-dr, -dc)))
        def _():
            got[first : first + count, :] = jnp.zeros((count, wide), BF16)

    pl.semaphore_wait(barrier, devices - 1)

    def halo(m):
        dr, dc = OFFSETS[m]
        first, count = block_rows(m)
        return pltpu.make_async_remote_copy(
            src_ref=sent.at[pl.ds(first, count)],
            dst_ref=got.at[pl.ds(first, count)],
            send_sem=halo_send.at[m],
            recv_sem=halo_recv.at[m],
            device_id=(row + dr, col + dc),
            device_id_type=MESH,
        )

    for m, (dr, dc) in enumerate(OFFSETS):
        @pl.when(inside_grid(dr, dc))
        def _():
            halo(m).start()

    placed = matmul(spread, one_hot(recvc[...], cells), ((1,), (1,))).astype(BF16)

    for name in names[5:9]:
        fetch(name).wait()

    for number in range(faces // chunk):
        at = number * chunk
        span = slice(at, at + chunk)
        span_b = slice(at + faces, at + faces + chunk)
        pair = facec[:, span]
        hot_a = one_hot(pair[0:1], cells)
        hot_b = one_hot(pair[1:2], cells)
        hot[:, span] = hot_a
        hot[:, span_b] = hot_b
        left = left_s.at[number % 2]
        right = right_s.at[number % 2]
        left[...] = matmul(flat, hot_a, ((1,), (0,)))
        right[...] = matmul(flat, hot_b, ((1,), (0,)))
        flag = flags[:, span].astype(F32)
        mark = jnp.where(
            lax.broadcasted_iota(jnp.int32, (16, chunk), 0) == 0, flag, 0.0
        ).astype(BF16)
        for side, values, where_to in ((0, right, span), (1, left, span_b)):
            for g in range(fields):
                total = None
                for f in range(fields):
                    entry = facej[g, f, side : side + 1, span]
                    if f == g:
                        entry = entry - visc[g] * flag
                    term = entry * values[f * modes : (f + 1) * modes, :]
                    total = term if total is None else total + term
                terms[g * modes : (g + 1) * modes, where_to] = total.astype(BF16)
            terms[wide : wide + 16, where_to] = mark

    image = matmul(terms[...], hot[...], ((1,), (1,)))
    for name in names[9:]:
        fetch(name).wait()
    flagged = image[wide : wide + 1, :]
    rows = []
    for g in range(fields):
        total = image[g * modes : (g + 1) * modes, :]
        for f in range(fields):
            entry = cellj[g, f : f + 1, :]
            if f == g:
                entry = entry + visc[g] * flagged
            total = total + entry * basis[f].astype(F32)
        rows.append(total)

    for m, (dr, dc) in enumerate(OFFSETS):
        @pl.when(inside_grid(-dr, -dc))
        def _():
            halo(m).wait_recv()

    arrived = matmul(got[...], placed, ((0,), (0,)))
    c = coords[...]
    high = c.astype(BF16).astype(F32)
    mid = (c - high).astype(BF16).astype(F32)
    low = c - high - mid
    sub16 = lax.broadcasted_iota(jnp.int32, (16, modes), 0)
    weights = jnp.where(
        sub16 == 0, high, jnp.where(sub16 == 1, mid, jnp.where(sub16 == 2, low, 0.0))
    ).astype(BF16)
    top = lax.broadcasted_iota(jnp.int32, (16, cells), 0) == 0
    gram = None

    def give(g):
        return pltpu.make_async_copy(
            stacked.at[g, pl.ds(0, modes)], tb_out.at[g], tb_sem.at[g]
        )

    images = [
        (rows[g] + arrived[g * modes : (g + 1) * modes]).astype(BF16) for g in range(fields)
    ]
    for g in range(fields):
        stacked[g, :modes, :] = images[g]
    for g in range(fields):
        shift = jnp.sum(matmul(weights, images[g], ((1,), (0,))), axis=0, keepdims=True)
        resid = base[g : g + 1, :] + row_scale * shift
        stacked[g, modes : modes + 16, :] = jnp.where(top, resid, 0.0).astype(BF16)
        stacked[g, modes + 16 :, :] = jnp.zeros((128 - modes - 16, cells), BF16)
    for g in range(fields):
        x = stacked[g]
        part = matmul(x, x, ((1,), (1,)))
        gram = part if gram is None else gram + part
    lane = lax.broadcasted_iota(jnp.int32, (8, 128), 1)
    for t in range(tiles):
        low = gram[8 * t : 8 * t + 8]
        u = last_tile - t
        if u > t:
            high = pltpu.roll(gram[8 * u : 8 * u + 8], 8 * (t + 1), 1)
            keep = (lane >= 8 * t) & (lane < 8 * (last_tile + 1))
            low = jnp.where(keep, low, high)
        gram_s[t] = low

    def owner(t):
        return (t * nrow) // tiles * ncol + (ncol - 1) // 2 + t % 2

    owns, tile = me == owner(0), jnp.int32(0)
    for t in range(1, tiles):
        owns = owns | (me == owner(t))
        tile = jnp.where(me == owner(t), t, tile)

    def up(t):
        o = owner(t)
        return pltpu.make_async_remote_copy(
            src_ref=gram_s.at[t],
            dst_ref=parts.at[me],
            send_sem=up_send,
            recv_sem=up_recv,
            device_id=(jnp.int32(o // ncol), jnp.int32(o % ncol)),
            device_id_type=MESH,
        )

    for t in range(tiles):
        @pl.when(me != owner(t))
        def _():
            up(t).start()

        @pl.when(me == owner(t))
        def _():
            parts[me] = gram_s[t]

    for g in range(fields):
        give(g).start()

    def many(ref, count, send_sem, recv_sem):
        return pltpu.make_async_remote_copy(
            src_ref=ref.at[pl.ds(0, count)],
            dst_ref=ref.at[pl.ds(0, count)],
            send_sem=send_sem,
            recv_sem=recv_sem,
            device_id=place(lax.rem(me + 1, jnp.int32(devices))),
            device_id_type=MESH,
        )

    @pl.when(owns)
    def _():
        many(parts, devices - 1, down_send, up_recv).wait_recv()
        total = jnp.sum(parts[...], axis=0)
        mine[...] = total
        summed[tile] = total

        for d in others:
            pltpu.make_async_remote_copy(
                src_ref=mine,
                dst_ref=summed.at[tile],
                send_sem=down_send,
                recv_sem=down_recv,
                device_id=place(d),
                device_id_type=MESH,
            ).start()

        many(summed, tiles - 1, up_send, down_recv).wait_recv()

    @pl.when(jnp.logical_not(owns))
    def _():
        many(summed, tiles, up_send, down_recv).wait_recv()

    gram_out[...] = summed[...]

    for g in range(fields):
        give(g).wait()

    for m, (dr, dc) in enumerate(OFFSETS):
        @pl.when(inside_grid(dr, dc))
        def _():
            halo(m).wait_send()

    @pl.when(owns)
    def _():
        many(gram_s, tiles - 1, up_send, up_recv).wait_send()
        many(parts, devices - 1, down_send, up_recv).wait_send()

    @pl.when(jnp.logical_not(owns))
    def _():
        many(gram_s, tiles, up_send, up_recv).wait_send()


def factor(modes, row_scale, gram, tb_in, upper, step, tb_out, held, sem):
    coming = pltpu.make_async_copy(tb_in, held, sem.at[0])
    going = pltpu.make_async_copy(held, tb_out, sem.at[1])
    coming.start()
    order = modes + 1
    tiles = (order + 7) // 8
    shape = (8, 128)
    sub = lax.broadcasted_iota(jnp.int32, shape, 0)
    lane = lax.broadcasted_iota(jnp.int32, shape, 1)

    def across(x, s):
        return jnp.broadcast_to(x[s : s + 1, :], shape)

    def along(x, c):
        return jnp.broadcast_to(x[:, c : c + 1], shape)

    half = []
    for t in range(tiles):
        u = tiles - 1 - t
        if t <= u:
            tile = gram[t]
        else:
            tile = pltpu.roll(gram[u], 128 - 8 * (u + 1), 1)
        half.append(jnp.where(lane >= sub + 8 * t, tile * (row_scale * row_scale), 0.0))
    full = jnp.concatenate(half + [jnp.zeros(shape, F32)] * (16 - tiles), axis=0)
    mirror = full.T
    rows = [
        jnp.where(lane >= sub + 8 * t, half[t], mirror[8 * t : 8 * t + 8]) for t in range(tiles)
    ]
    done = []
    for p in range(tiles):
        count = min(8, order - 8 * p)
        line = [across(rows[p], i) for i in range(count)]
        entry = {
            (i, k): along(line[i], 8 * p + k) for i in range(count) for k in range(i, count)
        }
        last = p == tiles - 1
        column = {
            t: [along(rows[t], 8 * p + j) for j in range(count)]
            for t in range(tiles) if t != p and not last
        }
        ahead = list(column[p + 1]) if not last else []
        factored, inverse, scaled = [], [], []
        for j in range(count):
            root = lax.rsqrt(entry[j, j])
            inverse.append(root * root)
            factored.append(line[j] * root)
            scaled.append(line[j] * inverse[j])
            for i in range(j + 1, count):
                ratio = entry[j, i] * inverse[j]
                for k in range(i, count):
                    entry[i, k] = entry[i, k] - ratio * entry[j, k]
                line[i] = line[i] - ratio * line[j]
                ahead[i] = ahead[i] - ratio * ahead[j]
        tile = factored[0]
        for j in range(1, count):
            tile = jnp.where(sub == j, factored[j], tile)
        done.append(tile)
        if last:
            break
        if p == 3:
            coming.wait()
            going.start()
        new = rows[p + 1]
        for j in range(count):
            new = new - ahead[j] * scaled[j]
        rows[p + 1] = new
        reduced = list(scaled)
        for j in range(count - 1, -1, -1):
            for k in range(j + 1, count):
                reduced[j] = reduced[j] - entry[j, k] * inverse[j] * reduced[k]
        for t in range(tiles):
            if t == p or t == p + 1:
                continue
            new = rows[t]
            for j in range(count):
                new = new - column[t][j] * reduced[j]
            rows[t] = new
        tile = reduced[0]
        for j in range(1, count):
            tile = jnp.where(sub == j, reduced[j], tile)
        rows[p] = tile
    solved = jnp.zeros(shape, F32)
    for t in range(tiles):
        kept = jnp.where(lane >= sub + 8 * t, done[t], 0.0)
        count = min(8, order - 8 * t)
        upper[8 * t : 8 * t + count, :] = kept[:count, :order]
        if 8 * t < modes:
            tail = along(rows[t], modes)
            solved = solved + jnp.where(lane == sub + 8 * t, tail, 0.0)
    step[...] = (jnp.sum(solved, axis=0, keepdims=True) * (-1.0 / row_scale))[:, :modes]
    going.wait()


def local(
    nrow, ncol,
    reduced_basis, cell_jacobian, face_cells, face_jacobian, limiter_flags, viscosity,
    ghost_cells, ghost_jacobian, ghost_counts, receive_cells, coordinates, base_residual,
):
    fields, modes, cells = reduced_basis.shape
    faces = face_cells.shape[1]
    devices = nrow * ncol
    wide = fields * modes
    row_scale = float((fields * cells * devices) ** (-0.5))
    blocks = (modes + 1 + 7) // 8
    tiles = (blocks + 1) // 2
    chunk = 256
    vmem = pl.BlockSpec(memory_space=pltpu.VMEM)
    hbm = pl.BlockSpec(memory_space=pltpu.HBM)
    dma = pltpu.SemaphoreType.DMA
    test_basis, gram = pl.pallas_call(
        functools.partial(assemble, nrow, ncol, row_scale, blocks - 1, tiles, chunk),
        out_shape=(
            jax.ShapeDtypeStruct((fields, modes, cells), BF16),
            jax.ShapeDtypeStruct((tiles, 8, 128), F32),
        ),
        in_specs=[hbm] * 12,
        out_specs=(hbm, vmem),
        scratch_shapes=[
            pltpu.VMEM((fields, modes, cells), BF16),
            pltpu.VMEM((fields, fields, cells), F32),
            pltpu.VMEM((2, faces), jnp.int32),
            pltpu.VMEM((fields, fields, 2, faces), F32),
            pltpu.VMEM((1, faces), jnp.int32),
            pltpu.SMEM((fields,), F32),
            pltpu.VMEM((1, SLOTS), jnp.int32),
            pltpu.VMEM((fields, fields, SLOTS), F32),
            pltpu.SMEM((8,), jnp.int32),
            pltpu.VMEM((1, SLOTS), jnp.int32),
            pltpu.VMEM((1, modes), F32),
            pltpu.VMEM((fields, cells), F32),
            dma((12,)),
            dma((fields,)),
            pltpu.VMEM((cells, 2 * faces), BF16),
            pltpu.VMEM((wide + 16, 2 * faces), BF16),
            pltpu.VMEM((2, wide, chunk), F32),
            pltpu.VMEM((2, wide, chunk), F32),
            pltpu.VMEM((SENT_ROWS, wide), BF16),
            pltpu.VMEM((SENT_ROWS, wide), BF16),
            pltpu.VMEM((fields, 128, cells), BF16),
            pltpu.VMEM((tiles, 8, 128), F32),
            pltpu.VMEM((devices, 8, 128), F32),
            pltpu.VMEM((8, 128), F32),
            pltpu.VMEM((tiles, 8, 128), F32),
            dma((8,)), dma((8,)), dma, dma, dma, dma,
        ],
        compiler_params=pltpu.CompilerParams(
            collective_id=0, has_side_effects=True, vmem_limit_bytes=64 * 1024 * 1024 - 65536
        ),
        cost_estimate=pl.CostEstimate(
            flops=8 * wide * cells * faces, bytes_accessed=3_000_000, transcendentals=0
        ),
        name="assemble",
    )(
        reduced_basis, cell_jacobian, face_cells, face_jacobian.transpose(1, 2, 0, 3),
        limiter_flags.reshape(1, -1),
        viscosity, ghost_cells.reshape(1, -1), ghost_jacobian, ghost_counts,
        receive_cells.reshape(1, -1), coordinates.reshape(1, -1), base_residual,
    )
    upper, step, test_basis = pl.pallas_call(
        functools.partial(factor, modes, row_scale),
        out_shape=(
            jax.ShapeDtypeStruct((modes + 1, modes + 1), F32),
            jax.ShapeDtypeStruct((1, modes), F32),
            jax.ShapeDtypeStruct((fields, modes, cells), BF16),
        ),
        in_specs=[vmem, hbm],
        out_specs=(vmem, vmem, hbm),
        scratch_shapes=[pltpu.VMEM((fields, modes, cells), BF16), dma((2,))],
        compiler_params=pltpu.CompilerParams(vmem_limit_bytes=64 * 1024 * 1024 - 65536),
        name="factor",
    )(gram, test_basis)
    return test_basis, upper, step.reshape(modes)


def solution(mesh):
    both = ("row", "col")
    placed = (
        P(None, None, both), P(None, None, both), P(None, both), P(None, None, None, both),
        P(both), P(), P(both), P(None, None, both), P(both), P(both), P(), P(None, both),
    )
    return jax.shard_map(
        functools.partial(local, mesh.shape["row"], mesh.shape["col"]),
        mesh=mesh,
        in_specs=placed,
        out_specs=(P(None, None, both), P(), P()),
        check_vma=False,
    )
```

```python
import functools

import jax
import jax.numpy as jnp
from jax import lax
from jax.experimental import pallas as pl
from jax.experimental.pallas import tpu as pltpu
from jax.sharding import PartitionSpec as P

FACE_CAP = 32
EDGE_CAP = 8
EDGE_ROWS = 16
OFFSETS = ((-1, 0), (1, 0), (0, -1), (0, 1), (-1, -1), (-1, 1), (1, -1), (1, 1))
SLOTS = 4 * FACE_CAP + 4 * EDGE_CAP
SENT_ROWS = 4 * FACE_CAP + 4 * EDGE_ROWS
MESH = pl.DeviceIdType.MESH
BF16 = jnp.bfloat16
F32 = jnp.float32


def block_rows(m):
    if m < 4:
        return m * FACE_CAP, FACE_CAP
    return 4 * FACE_CAP + (m - 4) * EDGE_ROWS, EDGE_ROWS


def one_hot(cells, count):
    rows = lax.broadcasted_iota(jnp.int32, (count, cells.shape[1]), 0)
    return jnp.where(rows == cells, 1.0, 0.0).astype(BF16)


def matmul(a, b, dims):
    return lax.dot_general(a, b, (dims, ((), ())), preferred_element_type=F32)


def assemble(
    nrow, ncol, row_scale, last_tile, tiles, chunk,
    basis_h, cellj_h, facec_h, facej_h, flags_h, visc_h, ghostc_h, ghostj_h, counts_h, recvc_h,
    coords_h, base_h,
    tb_out, gram_out,
    basis, cellj, facec, facej, flags, visc, ghostc, ghostj, counts, recvc, coords, base, in_sem,
    tb_sem, hot, terms, left_s, right_s, sent, got, stacked, gram_s, parts, mine, summed,
    halo_send, halo_recv, up_send, up_recv, down_send, down_recv,
):
    fields, modes, cells = basis.shape
    wide = fields * modes
    faces = facec.shape[1]
    devices = nrow * ncol
    row, col = lax.axis_index("row"), lax.axis_index("col")
    me = row * ncol + col

    def place(d):
        return (lax.div(d, jnp.int32(ncol)), lax.rem(d, jnp.int32(ncol)))

    names = ("basis", "ghostc", "counts", "ghostj", "recvc", "facec", "flags", "visc", "facej",
             "cellj", "coords", "base")
    inputs = dict(
        basis=(basis_h, basis), ghostc=(ghostc_h, ghostc), counts=(counts_h, counts),
        ghostj=(ghostj_h, ghostj), recvc=(recvc_h, recvc), facec=(facec_h, facec),
        flags=(flags_h, flags), visc=(visc_h, visc), facej=(facej_h, facej),
        cellj=(cellj_h, cellj), coords=(coords_h, coords), base=(base_h, base),
    )

    def fetch(name):
        return pltpu.make_async_copy(*inputs[name], in_sem.at[names.index(name)])

    for name in names:
        fetch(name).start()

    barrier = pltpu.get_barrier_semaphore()

    others = [lax.rem(me + k, jnp.int32(devices)) for k in range(1, devices)]
    for d in others:
        pl.semaphore_signal(barrier, inc=1, device_id=place(d), device_id_type=MESH)

    for name in names[:5]:
        fetch(name).wait()
    flat = basis[...].reshape(wide, cells)

    slot = lax.broadcasted_iota(jnp.int32, (1, SLOTS), 1)
    limit = jnp.zeros((1, SLOTS), jnp.int32)
    start = 0
    for m in range(8):
        width = FACE_CAP if m < 4 else EDGE_CAP
        inside = (slot >= start) & (slot < start + width)
        limit = jnp.where(inside, counts[m] + start, limit)
        start += width
    kept = slot < limit
    ghosts = matmul(flat, one_hot(ghostc[...], cells), ((1,), (0,)))
    pieces = []
    for g in range(fields):
        total = None
        for f in range(fields):
            entry = jnp.where(kept, ghostj[g, f : f + 1, :], 0.0)
            term = entry * ghosts[f * modes : (f + 1) * modes]
            total = term if total is None else total + term
        pieces.append(total.astype(BF16))
    partial = jnp.concatenate(pieces, axis=0)
    lane = lax.broadcasted_iota(jnp.int32, (SENT_ROWS, SLOTS), 1)
    sub = lax.broadcasted_iota(jnp.int32, (SENT_ROWS, SLOTS), 0)
    edge = lane - 4 * FACE_CAP
    target = jnp.where(edge < 0, lane, lane + (edge >> 3) * (EDGE_ROWS - EDGE_CAP))
    spread = jnp.where(sub == target, 1.0, 0.0).astype(BF16)
    sent[...] = matmul(spread, partial, ((1,), (1,))).astype(BF16)

    def inside_grid(dr, dc):
        ok = (row + dr >= 0) & (row + dr < nrow)
        return ok & (col + dc >= 0) & (col + dc < ncol)

    for m, (dr, dc) in enumerate(OFFSETS):
        first, count = block_rows(m)

        @pl.when(jnp.logical_not(inside_grid(-dr, -dc)))
        def _():
            got[first : first + count, :] = jnp.zeros((count, wide), BF16)

    pl.semaphore_wait(barrier, devices - 1)

    def halo(m):
        dr, dc = OFFSETS[m]
        first, count = block_rows(m)
        return pltpu.make_async_remote_copy(
            src_ref=sent.at[pl.ds(first, count)],
            dst_ref=got.at[pl.ds(first, count)],
            send_sem=halo_send.at[m],
            recv_sem=halo_recv.at[m],
            device_id=(row + dr, col + dc),
            device_id_type=MESH,
        )

    for m, (dr, dc) in enumerate(OFFSETS):
        @pl.when(inside_grid(dr, dc))
        def _():
            halo(m).start()

    placed = matmul(spread, one_hot(recvc[...], cells), ((1,), (1,))).astype(BF16)

    for name in names[5:9]:
        fetch(name).wait()

    for name in names[9:]:
        fetch(name).wait()
    own = []
    for g in range(fields):
        total = None
        for f in range(fields):
            term = cellj[g, f : f + 1, :] * basis[f].astype(F32)
            total = term if total is None else total + term
        own.append(total)

    image, first = None, 0
    for number in range(faces // chunk):
        at = number * chunk
        span = slice(at, at + chunk)
        span_a = slice(2 * at, 2 * at + chunk)
        span_b = slice(2 * at + chunk, 2 * at + 2 * chunk)
        pair = facec[:, span]
        hot_a = one_hot(pair[0:1], cells)
        hot_b = one_hot(pair[1:2], cells)
        hot[:, span_a] = hot_a
        hot[:, span_b] = hot_b
        left = left_s.at[number % 2]
        right = right_s.at[number % 2]
        left[...] = matmul(flat, hot_a, ((1,), (0,)))
        right[...] = matmul(flat, hot_b, ((1,), (0,)))
        flag = flags[:, span].astype(F32)
        mark = jnp.where(
            lax.broadcasted_iota(jnp.int32, (16, chunk), 0) == 0, flag, 0.0
        ).astype(BF16)
        for side, values, where_to in ((0, right, span_a), (1, left, span_b)):
            for g in range(fields):
                total = None
                for f in range(fields):
                    entry = facej[g, f, side : side + 1, span]
                    if f == g:
                        entry = entry - visc[g] * flag
                    term = entry * values[f * modes : (f + 1) * modes, :]
                    total = term if total is None else total + term
                terms[g * modes : (g + 1) * modes, where_to] = total.astype(BF16)
            terms[wide : wide + 16, where_to] = mark

        if 2 * (number + 1) == faces // chunk or number + 1 == faces // chunk:
            ready = slice(first, 2 * at + 2 * chunk)
            first = ready.stop
            part = matmul(terms[:, ready], hot[:, ready], ((1,), (1,)))
            image = part if image is None else image + part

    flagged = image[wide : wide + 1, :]
    rows = []
    for g in range(fields):
        total = own[g] + image[g * modes : (g + 1) * modes, :]
        rows.append(total + (visc[g] * flagged) * basis[g].astype(F32))

    for m, (dr, dc) in enumerate(OFFSETS):
        @pl.when(inside_grid(-dr, -dc))
        def _():
            halo(m).wait_recv()

    arrived = matmul(got[...], placed, ((0,), (0,)))
    c = coords[...]
    high = c.astype(BF16).astype(F32)
    mid = (c - high).astype(BF16).astype(F32)
    low = c - high - mid
    sub16 = lax.broadcasted_iota(jnp.int32, (16, modes), 0)
    weights = jnp.where(
        sub16 == 0, high, jnp.where(sub16 == 1, mid, jnp.where(sub16 == 2, low, 0.0))
    ).astype(BF16)
    top = lax.broadcasted_iota(jnp.int32, (16, cells), 0) == 0
    gram = None

    def give(g):
        return pltpu.make_async_copy(
            stacked.at[g, pl.ds(0, modes)], tb_out.at[g], tb_sem.at[g]
        )

    images = [
        (rows[g] + arrived[g * modes : (g + 1) * modes]).astype(BF16) for g in range(fields)
    ]
    for g in range(fields):
        stacked[g, :modes, :] = images[g]
    for g in range(fields):
        shift = jnp.sum(matmul(weights, images[g], ((1,), (0,))), axis=0, keepdims=True)
        resid = base[g : g + 1, :] + row_scale * shift
        stacked[g, modes : modes + 16, :] = jnp.where(top, resid, 0.0).astype(BF16)
        stacked[g, modes + 16 :, :] = jnp.zeros((128 - modes - 16, cells), BF16)
    for g in range(fields):
        x = stacked[g]
        part = matmul(x, x, ((1,), (1,)))
        gram = part if gram is None else gram + part
    lane = lax.broadcasted_iota(jnp.int32, (8, 128), 1)
    for t in range(tiles):
        low = gram[8 * t : 8 * t + 8]
        u = last_tile - t
        if u > t:
            high = pltpu.roll(gram[8 * u : 8 * u + 8], 8 * (t + 1), 1)
            keep = (lane >= 8 * t) & (lane < 8 * (last_tile + 1))
            low = jnp.where(keep, low, high)
        gram_s[t] = low

    def owner(t):
        return (t * nrow) // tiles * ncol + (ncol - 1) // 2 + t % 2

    owns, tile = me == owner(0), jnp.int32(0)
    for t in range(1, tiles):
        owns = owns | (me == owner(t))
        tile = jnp.where(me == owner(t), t, tile)

    def up(t):
        o = owner(t)
        return pltpu.make_async_remote_copy(
            src_ref=gram_s.at[t],
            dst_ref=parts.at[me],
            send_sem=up_send,
            recv_sem=up_recv,
            device_id=(jnp.int32(o // ncol), jnp.int32(o % ncol)),
            device_id_type=MESH,
        )

    for t in range(tiles):
        @pl.when(me != owner(t))
        def _():
            up(t).start()

        @pl.when(me == owner(t))
        def _():
            parts[me] = gram_s[t]

    for g in range(fields):
        give(g).start()

    def many(ref, count, send_sem, recv_sem):
        return pltpu.make_async_remote_copy(
            src_ref=ref.at[pl.ds(0, count)],
            dst_ref=ref.at[pl.ds(0, count)],
            send_sem=send_sem,
            recv_sem=recv_sem,
            device_id=place(lax.rem(me + 1, jnp.int32(devices))),
            device_id_type=MESH,
        )

    @pl.when(owns)
    def _():
        many(parts, devices - 1, down_send, up_recv).wait_recv()
        total = jnp.sum(parts[...], axis=0)
        mine[...] = total
        summed[tile] = total

        for d in others:
            pltpu.make_async_remote_copy(
                src_ref=mine,
                dst_ref=summed.at[tile],
                send_sem=down_send,
                recv_sem=down_recv,
                device_id=place(d),
                device_id_type=MESH,
            ).start()

        many(summed, tiles - 1, up_send, down_recv).wait_recv()

    @pl.when(jnp.logical_not(owns))
    def _():
        many(summed, tiles, up_send, down_recv).wait_recv()

    gram_out[...] = summed[...]

    for g in range(fields):
        give(g).wait()

    for m, (dr, dc) in enumerate(OFFSETS):
        @pl.when(inside_grid(dr, dc))
        def _():
            halo(m).wait_send()

    @pl.when(owns)
    def _():
        many(gram_s, tiles - 1, up_send, up_recv).wait_send()
        many(parts, devices - 1, down_send, up_recv).wait_send()

    @pl.when(jnp.logical_not(owns))
    def _():
        many(gram_s, tiles, up_send, up_recv).wait_send()


def factor(modes, row_scale, gram, tb_in, upper, step, tb_out, held, sem):
    coming = pltpu.make_async_copy(tb_in, held, sem.at[0])
    going = pltpu.make_async_copy(held, tb_out, sem.at[1])
    coming.start()
    order = modes + 1
    tiles = (order + 7) // 8
    shape = (8, 128)
    sub = lax.broadcasted_iota(jnp.int32, shape, 0)
    lane = lax.broadcasted_iota(jnp.int32, shape, 1)

    def across(x, s):
        return jnp.broadcast_to(x[s : s + 1, :], shape)

    def along(x, c):
        return jnp.broadcast_to(x[:, c : c + 1], shape)

    half = []
    for t in range(tiles):
        u = tiles - 1 - t
        if t <= u:
            tile = gram[t]
        else:
            tile = pltpu.roll(gram[u], 128 - 8 * (u + 1), 1)
        half.append(jnp.where(lane >= sub + 8 * t, tile * (row_scale * row_scale), 0.0))
    full = jnp.concatenate(half + [jnp.zeros(shape, F32)] * (16 - tiles), axis=0)
    mirror = full.T
    rows = [
        jnp.where(lane >= sub + 8 * t, half[t], mirror[8 * t : 8 * t + 8]) for t in range(tiles)
    ]
    done = []
    for p in range(tiles):
        count = min(8, order - 8 * p)
        line = [across(rows[p], i) for i in range(count)]
        entry = {
            (i, k): along(line[i], 8 * p + k) for i in range(count) for k in range(i, count)
        }
        last = p == tiles - 1
        column = {
            t: [along(rows[t], 8 * p + j) for j in range(count)]
            for t in range(tiles) if t != p and not last
        }
        ahead = list(column[p + 1]) if not last else []
        factored, inverse, scaled = [], [], []
        for j in range(count):
            root = lax.rsqrt(entry[j, j])
            inverse.append(root * root)
            factored.append(line[j] * root)
            scaled.append(line[j] * inverse[j])
            for i in range(j + 1, count):
                ratio = entry[j, i] * inverse[j]
                for k in range(i, count):
                    entry[i, k] = entry[i, k] - (entry[j, i] * entry[j, k]) * inverse[j]
                line[i] = line[i] - ratio * line[j]
                ahead[i] = ahead[i] - ratio * ahead[j]
        tile = factored[0]
        for j in range(1, count):
            tile = jnp.where(sub == j, factored[j], tile)
        done.append(tile)
        if last:
            break
        if p == 3:
            coming.wait()
            going.start()
        new = rows[p + 1]
        for j in range(count):
            new = new - ahead[j] * scaled[j]
        rows[p + 1] = new
        reduced = list(scaled)
        for j in range(count - 1, -1, -1):
            for k in range(j + 1, count):
                reduced[j] = reduced[j] - entry[j, k] * inverse[j] * reduced[k]
        for t in range(tiles):
            if t == p or t == p + 1:
                continue
            new = rows[t]
            for j in range(count):
                new = new - column[t][j] * reduced[j]
            rows[t] = new
        tile = reduced[0]
        for j in range(1, count):
            tile = jnp.where(sub == j, reduced[j], tile)
        rows[p] = tile
    solved = jnp.zeros(shape, F32)
    for t in range(tiles):
        kept = jnp.where(lane >= sub + 8 * t, done[t], 0.0)
        count = min(8, order - 8 * t)
        upper[8 * t : 8 * t + count, :] = kept[:count, :order]
        if 8 * t < modes:
            tail = along(rows[t], modes)
            solved = solved + jnp.where(lane == sub + 8 * t, tail, 0.0)
    step[...] = (jnp.sum(solved, axis=0, keepdims=True) * (-1.0 / row_scale))[:, :modes]
    going.wait()


def local(
    nrow, ncol,
    reduced_basis, cell_jacobian, face_cells, face_jacobian, limiter_flags, viscosity,
    ghost_cells, ghost_jacobian, ghost_counts, receive_cells, coordinates, base_residual,
):
    fields, modes, cells = reduced_basis.shape
    faces = face_cells.shape[1]
    devices = nrow * ncol
    wide = fields * modes
    row_scale = float((fields * cells * devices) ** (-0.5))
    blocks = (modes + 1 + 7) // 8
    tiles = (blocks + 1) // 2
    chunk = 256
    vmem = pl.BlockSpec(memory_space=pltpu.VMEM)
    hbm = pl.BlockSpec(memory_space=pltpu.HBM)
    dma = pltpu.SemaphoreType.DMA
    test_basis, gram = pl.pallas_call(
        functools.partial(assemble, nrow, ncol, row_scale, blocks - 1, tiles, chunk),
        out_shape=(
            jax.ShapeDtypeStruct((fields, modes, cells), BF16),
            jax.ShapeDtypeStruct((tiles, 8, 128), F32),
        ),
        in_specs=[hbm] * 12,
        out_specs=(hbm, vmem),
        scratch_shapes=[
            pltpu.VMEM((fields, modes, cells), BF16),
            pltpu.VMEM((fields, fields, cells), F32),
            pltpu.VMEM((2, faces), jnp.int32),
            pltpu.VMEM((fields, fields, 2, faces), F32),
            pltpu.VMEM((1, faces), jnp.int32),
            pltpu.SMEM((fields,), F32),
            pltpu.VMEM((1, SLOTS), jnp.int32),
            pltpu.VMEM((fields, fields, SLOTS), F32),
            pltpu.SMEM((8,), jnp.int32),
            pltpu.VMEM((1, SLOTS), jnp.int32),
            pltpu.VMEM((1, modes), F32),
            pltpu.VMEM((fields, cells), F32),
            dma((12,)),
            dma((fields,)),
            pltpu.VMEM((cells, 2 * faces), BF16),
            pltpu.VMEM((wide + 16, 2 * faces), BF16),
            pltpu.VMEM((2, wide, chunk), F32),
            pltpu.VMEM((2, wide, chunk), F32),
            pltpu.VMEM((SENT_ROWS, wide), BF16),
            pltpu.VMEM((SENT_ROWS, wide), BF16),
            pltpu.VMEM((fields, 128, cells), BF16),
            pltpu.VMEM((tiles, 8, 128), F32),
            pltpu.VMEM((devices, 8, 128), F32),
            pltpu.VMEM((8, 128), F32),
            pltpu.VMEM((tiles, 8, 128), F32),
            dma((8,)), dma((8,)), dma, dma, dma, dma,
        ],
        compiler_params=pltpu.CompilerParams(
            collective_id=0, has_side_effects=True, vmem_limit_bytes=64 * 1024 * 1024 - 65536
        ),
        cost_estimate=pl.CostEstimate(
            flops=8 * wide * cells * faces, bytes_accessed=3_000_000, transcendentals=0
        ),
        name="assemble",
    )(
        reduced_basis, cell_jacobian, face_cells, face_jacobian.transpose(1, 2, 0, 3),
        limiter_flags.reshape(1, -1),
        viscosity, ghost_cells.reshape(1, -1), ghost_jacobian, ghost_counts,
        receive_cells.reshape(1, -1), coordinates.reshape(1, -1), base_residual,
    )
    upper, step, test_basis = pl.pallas_call(
        functools.partial(factor, modes, row_scale),
        out_shape=(
            jax.ShapeDtypeStruct((modes + 1, modes + 1), F32),
            jax.ShapeDtypeStruct((1, modes), F32),
            jax.ShapeDtypeStruct((fields, modes, cells), BF16),
        ),
        in_specs=[vmem, hbm],
        out_specs=(vmem, vmem, hbm),
        scratch_shapes=[pltpu.VMEM((fields, modes, cells), BF16), dma((2,))],
        compiler_params=pltpu.CompilerParams(vmem_limit_bytes=64 * 1024 * 1024 - 65536),
        name="factor",
    )(gram, test_basis)
    return test_basis, upper, step.reshape(modes)


def solution(mesh):
    both = ("row", "col")
    placed = (
        P(None, None, both), P(None, None, both), P(None, both), P(None, None, None, both),
        P(both), P(), P(both), P(None, None, both), P(both), P(both), P(), P(None, both),
    )
    return jax.shard_map(
        functools.partial(local, mesh.shape["row"], mesh.shape["col"]),
        mesh=mesh,
        in_specs=placed,
        out_specs=(P(None, None, both), P(), P()),
        check_vma=False,
    )
```

```python
import functools

import jax
import jax.numpy as jnp
from jax import lax
from jax.experimental import pallas as pl
from jax.experimental.pallas import tpu as pltpu
from jax.sharding import PartitionSpec as P

FACE_CAP = 32
EDGE_CAP = 8
EDGE_ROWS = 16
OFFSETS = ((-1, 0), (1, 0), (0, -1), (0, 1), (-1, -1), (-1, 1), (1, -1), (1, 1))
SLOTS = 4 * FACE_CAP + 4 * EDGE_CAP
SENT_ROWS = 4 * FACE_CAP + 4 * EDGE_ROWS
MESH = pl.DeviceIdType.MESH
BF16 = jnp.bfloat16
F32 = jnp.float32


def block_rows(m):
    if m < 4:
        return m * FACE_CAP, FACE_CAP
    return 4 * FACE_CAP + (m - 4) * EDGE_ROWS, EDGE_ROWS


def one_hot(cells, count):
    rows = lax.broadcasted_iota(jnp.int32, (count, cells.shape[1]), 0)
    return jnp.where(rows == cells, 1.0, 0.0).astype(BF16)


def matmul(a, b, dims):
    return lax.dot_general(a, b, (dims, ((), ())), preferred_element_type=F32)


def assemble(
    nrow, ncol, row_scale, last_tile, tiles, chunk,
    basis_h, cellj_h, facec_h, facej_h, flags_h, visc_h, ghostc_h, ghostj_h, counts_h, recvc_h,
    coords_h, base_h,
    tb_out, gram_out,
    basis, cellj, facec, facej, flags, visc, ghostc, ghostj, counts, recvc, coords, base, in_sem,
    tb_sem, hot, terms, left_s, right_s, sent, got, stacked, gram_s, parts, mine, summed,
    halo_send, halo_recv, up_send, up_recv, down_send, down_recv,
):
    fields, modes, cells = basis.shape
    wide = fields * modes
    faces = facec.shape[1]
    devices = nrow * ncol
    row, col = lax.axis_index("row"), lax.axis_index("col")
    me = row * ncol + col

    def place(d):
        return (lax.div(d, jnp.int32(ncol)), lax.rem(d, jnp.int32(ncol)))

    names = ("facec", "ghostc", "basis", "counts", "ghostj", "recvc", "flags", "visc", "facej",
             "cellj", "coords", "base")
    inputs = dict(
        basis=(basis_h, basis), ghostc=(ghostc_h, ghostc), counts=(counts_h, counts),
        ghostj=(ghostj_h, ghostj), recvc=(recvc_h, recvc), facec=(facec_h, facec),
        flags=(flags_h, flags), visc=(visc_h, visc), facej=(facej_h, facej),
        cellj=(cellj_h, cellj), coords=(coords_h, coords), base=(base_h, base),
    )

    def fetch(name):
        return pltpu.make_async_copy(*inputs[name], in_sem.at[names.index(name)])

    for name in names:
        fetch(name).start()

    barrier = pltpu.get_barrier_semaphore()

    others = [lax.rem(me + k, jnp.int32(devices)) for k in range(1, devices)]
    for d in others:
        pl.semaphore_signal(barrier, inc=1, device_id=place(d), device_id_type=MESH)

    fetch(names[0]).wait()
    for at in range(0, faces, chunk):
        for side in range(2):
            pair = facec[side : side + 1, at : at + chunk]
            hot[:, side * faces + at : side * faces + at + chunk] = one_hot(pair, cells)

    for name in names[1:6]:
        fetch(name).wait()
    flat = basis[...].reshape(wide, cells)

    slot = lax.broadcasted_iota(jnp.int32, (1, SLOTS), 1)
    limit = jnp.zeros((1, SLOTS), jnp.int32)
    start = 0
    for m in range(8):
        width = FACE_CAP if m < 4 else EDGE_CAP
        inside = (slot >= start) & (slot < start + width)
        limit = jnp.where(inside, counts[m] + start, limit)
        start += width
    kept = slot < limit
    ghosts = matmul(flat, one_hot(ghostc[...], cells), ((1,), (0,)))
    pieces = []
    for g in range(fields):
        total = None
        for f in range(fields):
            entry = jnp.where(kept, ghostj[g, f : f + 1, :], 0.0)
            term = entry * ghosts[f * modes : (f + 1) * modes]
            total = term if total is None else total + term
        pieces.append(total.astype(BF16))
    partial = jnp.concatenate(pieces, axis=0)
    lane = lax.broadcasted_iota(jnp.int32, (SENT_ROWS, SLOTS), 1)
    sub = lax.broadcasted_iota(jnp.int32, (SENT_ROWS, SLOTS), 0)
    edge = lane - 4 * FACE_CAP
    target = jnp.where(edge < 0, lane, lane + (edge >> 3) * (EDGE_ROWS - EDGE_CAP))
    spread = jnp.where(sub == target, 1.0, 0.0).astype(BF16)
    sent[...] = matmul(spread, partial, ((1,), (1,))).astype(BF16)

    def inside_grid(dr, dc):
        ok = (row + dr >= 0) & (row + dr < nrow)
        return ok & (col + dc >= 0) & (col + dc < ncol)

    for m, (dr, dc) in enumerate(OFFSETS):
        first, count = block_rows(m)

        @pl.when(jnp.logical_not(inside_grid(-dr, -dc)))
        def _():
            got[first : first + count, :] = jnp.zeros((count, wide), BF16)

    pl.semaphore_wait(barrier, devices - 1)

    def halo(m):
        dr, dc = OFFSETS[m]
        first, count = block_rows(m)
        return pltpu.make_async_remote_copy(
            src_ref=sent.at[pl.ds(first, count)],
            dst_ref=got.at[pl.ds(first, count)],
            send_sem=halo_send.at[m],
            recv_sem=halo_recv.at[m],
            device_id=(row + dr, col + dc),
            device_id_type=MESH,
        )

    for m, (dr, dc) in enumerate(OFFSETS):
        @pl.when(inside_grid(dr, dc))
        def _():
            halo(m).start()

    placed = matmul(spread, one_hot(recvc[...], cells), ((1,), (1,))).astype(BF16)

    for name in names[6:9]:
        fetch(name).wait()

    for number in range(faces // chunk):
        at = number * chunk
        span = slice(at, at + chunk)
        span_b = slice(at + faces, at + faces + chunk)
        left = left_s.at[number % 2]
        right = right_s.at[number % 2]
        left[...] = matmul(flat, hot[:, span], ((1,), (0,)))
        right[...] = matmul(flat, hot[:, span_b], ((1,), (0,)))
        flag = flags[:, span].astype(F32)
        mark = jnp.where(
            lax.broadcasted_iota(jnp.int32, (16, chunk), 0) == 0, flag, 0.0
        ).astype(BF16)
        for side, values, where_to in ((0, right, span), (1, left, span_b)):
            for g in range(fields):
                total = None
                for f in range(fields):
                    entry = facej[g, f, side : side + 1, span]
                    if f == g:
                        entry = entry - visc[g] * flag
                    term = entry * values[f * modes : (f + 1) * modes, :]
                    total = term if total is None else total + term
                terms[g * modes : (g + 1) * modes, where_to] = total.astype(BF16)
            terms[wide : wide + 16, where_to] = mark

    image = matmul(terms[...], hot[...], ((1,), (1,)))
    for name in names[9:]:
        fetch(name).wait()
    flagged = image[wide : wide + 1, :]
    rows = []
    for g in range(fields):
        total = image[g * modes : (g + 1) * modes, :]
        for f in range(fields):
            entry = cellj[g, f : f + 1, :]
            if f == g:
                entry = entry + visc[g] * flagged
            total = total + entry * basis[f].astype(F32)
        rows.append(total)

    for m, (dr, dc) in enumerate(OFFSETS):
        @pl.when(inside_grid(-dr, -dc))
        def _():
            halo(m).wait_recv()

    arrived = matmul(got[...], placed, ((0,), (0,)))
    c = coords[...]
    high = c.astype(BF16).astype(F32)
    mid = (c - high).astype(BF16).astype(F32)
    low = c - high - mid
    sub16 = lax.broadcasted_iota(jnp.int32, (16, modes), 0)
    weights = jnp.where(
        sub16 == 0, high, jnp.where(sub16 == 1, mid, jnp.where(sub16 == 2, low, 0.0))
    ).astype(BF16)
    top = lax.broadcasted_iota(jnp.int32, (16, cells), 0) == 0
    gram = None

    def give(g):
        return pltpu.make_async_copy(
            stacked.at[g, pl.ds(0, modes)], tb_out.at[g], tb_sem.at[g]
        )

    images = [
        (rows[g] + arrived[g * modes : (g + 1) * modes]).astype(BF16) for g in range(fields)
    ]
    for g in range(fields):
        stacked[g, :modes, :] = images[g]
    for g in range(fields):
        shift = jnp.sum(matmul(weights, images[g], ((1,), (0,))), axis=0, keepdims=True)
        resid = base[g : g + 1, :] + row_scale * shift
        stacked[g, modes : modes + 16, :] = jnp.where(top, resid, 0.0).astype(BF16)
        stacked[g, modes + 16 :, :] = jnp.zeros((128 - modes - 16, cells), BF16)
    for g in range(fields):
        x = stacked[g]
        part = matmul(x, x, ((1,), (1,)))
        gram = part if gram is None else gram + part
    lane = lax.broadcasted_iota(jnp.int32, (8, 128), 1)
    for t in range(tiles):
        low = gram[8 * t : 8 * t + 8]
        u = last_tile - t
        if u > t:
            high = pltpu.roll(gram[8 * u : 8 * u + 8], 8 * (t + 1), 1)
            keep = (lane >= 8 * t) & (lane < 8 * (last_tile + 1))
            low = jnp.where(keep, low, high)
        gram_s[t] = low

    def owner(t):
        return (t * nrow) // tiles * ncol + (ncol - 1) // 2 + t % 2

    owns, tile = me == owner(0), jnp.int32(0)
    for t in range(1, tiles):
        owns = owns | (me == owner(t))
        tile = jnp.where(me == owner(t), t, tile)

    def up(t):
        o = owner(t)
        return pltpu.make_async_remote_copy(
            src_ref=gram_s.at[t],
            dst_ref=parts.at[me],
            send_sem=up_send,
            recv_sem=up_recv,
            device_id=(jnp.int32(o // ncol), jnp.int32(o % ncol)),
            device_id_type=MESH,
        )

    for t in range(tiles):
        @pl.when(me != owner(t))
        def _():
            up(t).start()

        @pl.when(me == owner(t))
        def _():
            parts[me] = gram_s[t]

    for g in range(fields):
        give(g).start()

    def many(ref, count, send_sem, recv_sem):
        return pltpu.make_async_remote_copy(
            src_ref=ref.at[pl.ds(0, count)],
            dst_ref=ref.at[pl.ds(0, count)],
            send_sem=send_sem,
            recv_sem=recv_sem,
            device_id=place(lax.rem(me + 1, jnp.int32(devices))),
            device_id_type=MESH,
        )

    @pl.when(owns)
    def _():
        many(parts, devices - 1, down_send, up_recv).wait_recv()
        total = jnp.sum(parts[...], axis=0)
        mine[...] = total
        summed[tile] = total

        for d in others:
            pltpu.make_async_remote_copy(
                src_ref=mine,
                dst_ref=summed.at[tile],
                send_sem=down_send,
                recv_sem=down_recv,
                device_id=place(d),
                device_id_type=MESH,
            ).start()

        many(summed, tiles - 1, up_send, down_recv).wait_recv()

    @pl.when(jnp.logical_not(owns))
    def _():
        many(summed, tiles, up_send, down_recv).wait_recv()

    gram_out[...] = summed[...]

    for g in range(fields):
        give(g).wait()

    for m, (dr, dc) in enumerate(OFFSETS):
        @pl.when(inside_grid(dr, dc))
        def _():
            halo(m).wait_send()

    @pl.when(owns)
    def _():
        many(gram_s, tiles - 1, up_send, up_recv).wait_send()
        many(parts, devices - 1, down_send, up_recv).wait_send()

    @pl.when(jnp.logical_not(owns))
    def _():
        many(gram_s, tiles, up_send, up_recv).wait_send()


def factor(modes, row_scale, gram, tb_in, upper, step, tb_out, held, sem):
    coming = pltpu.make_async_copy(tb_in, held, sem.at[0])
    going = pltpu.make_async_copy(held, tb_out, sem.at[1])
    coming.start()
    order = modes + 1
    tiles = (order + 7) // 8
    shape = (8, 128)
    sub = lax.broadcasted_iota(jnp.int32, shape, 0)
    lane = lax.broadcasted_iota(jnp.int32, shape, 1)

    def across(x, s):
        return jnp.broadcast_to(x[s : s + 1, :], shape)

    def along(x, c):
        return jnp.broadcast_to(x[:, c : c + 1], shape)

    half = []
    for t in range(tiles):
        u = tiles - 1 - t
        if t <= u:
            tile = gram[t]
        else:
            tile = pltpu.roll(gram[u], 128 - 8 * (u + 1), 1)
        half.append(jnp.where(lane >= sub + 8 * t, tile * (row_scale * row_scale), 0.0))
    full = jnp.concatenate(half + [jnp.zeros(shape, F32)] * (16 - tiles), axis=0)
    mirror = full.T
    rows = [
        jnp.where(lane >= sub + 8 * t, half[t], mirror[8 * t : 8 * t + 8]) for t in range(tiles)
    ]
    done = []
    for p in range(tiles):
        count = min(8, order - 8 * p)
        line = [across(rows[p], i) for i in range(count)]
        spread = [along(rows[p], 8 * p + k) for k in range(count)]
        entry = {
            (i, k): across(spread[k], i) for i in range(count) for k in range(i, count)
        }
        last = p == tiles - 1
        column = {
            t: [along(rows[t], 8 * p + j) for j in range(count)]
            for t in range(tiles) if t != p and not last
        }
        ahead = list(column[p + 1]) if not last else []
        factored, inverse, scaled = [], [], []
        for j in range(count):
            root = lax.rsqrt(entry[j, j])
            inverse.append(root * root)
            factored.append(line[j] * root)
            scaled.append(line[j] * inverse[j])
            for i in range(j + 1, count):
                ratio = entry[j, i] * inverse[j]
                for k in range(i, count):
                    entry[i, k] = entry[i, k] - ratio * entry[j, k]
                line[i] = line[i] - ratio * line[j]
                ahead[i] = ahead[i] - ratio * ahead[j]
        tile = factored[0]
        for j in range(1, count):
            tile = jnp.where(sub == j, factored[j], tile)
        done.append(tile)
        if last:
            break
        if p == 3:
            coming.wait()
            going.start()
        new = rows[p + 1]
        for j in range(count):
            new = new - ahead[j] * scaled[j]
        rows[p + 1] = new
        reduced = list(scaled)
        for j in range(count - 1, -1, -1):
            for k in range(j + 1, count):
                reduced[j] = reduced[j] - entry[j, k] * inverse[j] * reduced[k]
        for t in range(tiles):
            if t == p or t == p + 1:
                continue
            new = rows[t]
            for j in range(count):
                new = new - column[t][j] * reduced[j]
            rows[t] = new
        tile = reduced[0]
        for j in range(1, count):
            tile = jnp.where(sub == j, reduced[j], tile)
        rows[p] = tile
    solved = jnp.zeros(shape, F32)
    for t in range(tiles):
        kept = jnp.where(lane >= sub + 8 * t, done[t], 0.0)
        count = min(8, order - 8 * t)
        upper[8 * t : 8 * t + count, :] = kept[:count, :order]
        if 8 * t < modes:
            tail = along(rows[t], modes)
            solved = solved + jnp.where(lane == sub + 8 * t, tail, 0.0)
    step[...] = (jnp.sum(solved, axis=0, keepdims=True) * (-1.0 / row_scale))[:, :modes]
    going.wait()


def local(
    nrow, ncol,
    reduced_basis, cell_jacobian, face_cells, face_jacobian, limiter_flags, viscosity,
    ghost_cells, ghost_jacobian, ghost_counts, receive_cells, coordinates, base_residual,
):
    fields, modes, cells = reduced_basis.shape
    faces = face_cells.shape[1]
    devices = nrow * ncol
    wide = fields * modes
    row_scale = float((fields * cells * devices) ** (-0.5))
    blocks = (modes + 1 + 7) // 8
    tiles = (blocks + 1) // 2
    chunk = 256
    vmem = pl.BlockSpec(memory_space=pltpu.VMEM)
    hbm = pl.BlockSpec(memory_space=pltpu.HBM)
    dma = pltpu.SemaphoreType.DMA
    test_basis, gram = pl.pallas_call(
        functools.partial(assemble, nrow, ncol, row_scale, blocks - 1, tiles, chunk),
        out_shape=(
            jax.ShapeDtypeStruct((fields, modes, cells), BF16),
            jax.ShapeDtypeStruct((tiles, 8, 128), F32),
        ),
        in_specs=[hbm] * 12,
        out_specs=(hbm, vmem),
        scratch_shapes=[
            pltpu.VMEM((fields, modes, cells), BF16),
            pltpu.VMEM((fields, fields, cells), F32),
            pltpu.VMEM((2, faces), jnp.int32),
            pltpu.VMEM((fields, fields, 2, faces), F32),
            pltpu.VMEM((1, faces), jnp.int32),
            pltpu.SMEM((fields,), F32),
            pltpu.VMEM((1, SLOTS), jnp.int32),
            pltpu.VMEM((fields, fields, SLOTS), F32),
            pltpu.SMEM((8,), jnp.int32),
            pltpu.VMEM((1, SLOTS), jnp.int32),
            pltpu.VMEM((1, modes), F32),
            pltpu.VMEM((fields, cells), F32),
            dma((12,)),
            dma((fields,)),
            pltpu.VMEM((cells, 2 * faces), BF16),
            pltpu.VMEM((wide + 16, 2 * faces), BF16),
            pltpu.VMEM((2, wide, chunk), F32),
            pltpu.VMEM((2, wide, chunk), F32),
            pltpu.VMEM((SENT_ROWS, wide), BF16),
            pltpu.VMEM((SENT_ROWS, wide), BF16),
            pltpu.VMEM((fields, 128, cells), BF16),
            pltpu.VMEM((tiles, 8, 128), F32),
            pltpu.VMEM((devices, 8, 128), F32),
            pltpu.VMEM((8, 128), F32),
            pltpu.VMEM((tiles, 8, 128), F32),
            dma((8,)), dma((8,)), dma, dma, dma, dma,
        ],
        compiler_params=pltpu.CompilerParams(
            collective_id=0, has_side_effects=True, vmem_limit_bytes=64 * 1024 * 1024 - 65536
        ),
        cost_estimate=pl.CostEstimate(
            flops=8 * wide * cells * faces, bytes_accessed=3_000_000, transcendentals=0
        ),
        name="assemble",
    )(
        reduced_basis, cell_jacobian, face_cells, face_jacobian.transpose(1, 2, 0, 3),
        limiter_flags.reshape(1, -1),
        viscosity, ghost_cells.reshape(1, -1), ghost_jacobian, ghost_counts,
        receive_cells.reshape(1, -1), coordinates.reshape(1, -1), base_residual,
    )
    upper, step, test_basis = pl.pallas_call(
        functools.partial(factor, modes, row_scale),
        out_shape=(
            jax.ShapeDtypeStruct((modes + 1, modes + 1), F32),
            jax.ShapeDtypeStruct((1, modes), F32),
            jax.ShapeDtypeStruct((fields, modes, cells), BF16),
        ),
        in_specs=[vmem, hbm],
        out_specs=(vmem, vmem, hbm),
        scratch_shapes=[pltpu.VMEM((fields, modes, cells), BF16), dma((2,))],
        compiler_params=pltpu.CompilerParams(vmem_limit_bytes=64 * 1024 * 1024 - 65536),
        name="factor",
    )(gram, test_basis)
    return test_basis, upper, step.reshape(modes)


def solution(mesh):
    both = ("row", "col")
    placed = (
        P(None, None, both), P(None, None, both), P(None, both), P(None, None, None, both),
        P(both), P(), P(both), P(None, None, both), P(both), P(both), P(), P(None, both),
    )
    return jax.shard_map(
        functools.partial(local, mesh.shape["row"], mesh.shape["col"]),
        mesh=mesh,
        in_specs=placed,
        out_specs=(P(None, None, both), P(), P()),
        check_vma=False,
    )
```
